256 devices in a mesh: dp: 8 (over z), expert: 32 (over x, y, core).
Axes of the slice: x: 4, y: 4, z: 8, core: 2. Of those that a mesh axis runs over, the one named last changes fastest.
Arguments:
- tokens: bfloat16 [2048, 7168], P('expert', 'dp'), may hold values from -6 to 6
- tangent: bfloat16 [2048, 7168], P('expert', 'dp'), may hold values from -6 to 6
- cotangent: bfloat16 [2048, 7168], P('expert', 'dp'), may hold values from -3 to 3
- routing: int32 [2048, 8], P('expert'), may hold values from 0 to 31, all different within a row; in each aligned block of 64 rows (0 to 63, 64 to 127, ...) at most 18 rows name the same one
- gate_weights: float32 [2048, 8], P('expert'), may hold values from 0.1 to 0.6
- gate_proj: bfloat16 [32, 7168, 2048], P('expert', 'dp'), may hold values from -0.0625 to 0.0625
- up_proj: bfloat16 [32, 7168, 2048], P('expert', 'dp'), may hold values from -0.0625 to 0.0625
- down_proj: bfloat16 [32, 2048, 7168], P('expert', None, 'dp'), may hold values from -0.125 to 0.125
Outputs:
- hessian_product: float32 [2048, 7168], P('expert', 'dp')
The draws below stay inside these ranges and needn't reach their ends.
Inputs may be any that keep to these rules, and one draw needn't show every extreme that they name: `routing`: each token names 8 different experts. In each aligned block of 64 tokens (the tokens of one index of expert) no expert is named more than 18 times, a bound that some block reaches.
All inputs are finite; a program needn't handle non-finite values.
Results may differ from the reference program's by a relative error of at most 0.0041.
Values may be sent and summed in bfloat16 or wider, within the bound.
A program may use at most 128 MiB of HBM per device.

```python
import math
import jax
import jax.numpy as jnp
import numpy as np
from jax import lax

D = 7168
H = 2048
TOP = 8
TOK_DEV = 64
EXPERTS = 32
CAP = 18
TOKENS = 2048
N_EXPERT = 32


def level_of(own_key, shape, cuts, least, high):
    level = 1.0
    for axis_at, blocks in cuts:
        heights = jax.random.uniform(jax.random.fold_in(jax.random.fold_in(own_key, 6), axis_at), (blocks,), jnp.float32, least / len(cuts), high / len(cuts))
        level = level * jnp.repeat(jnp.exp(heights), shape[axis_at] // blocks).reshape((-1,) + (1,) * (len(shape) - 1 - axis_at))
    return level


def assign_block(key, own, number, rows, number_of, top, limit, slope):
    order = jax.random.permutation(key, number_of)
    packed, ordinary = portions_of(number_of, rows * top, limit, slope, True), portions_of(number_of, rows * top, limit, slope, False)
    places = jnp.arange(number_of)

    def named(sizes, offset_by):
        used = int((sizes > 0).sum())
        fixed = max(1, used // 4)
        shifted = fixed + (places - fixed + offset_by * (used - fixed)) % max(1, number_of - fixed)
        return jnp.zeros((number_of,), jnp.int32).at[order[jnp.where(places < fixed, places, shifted)]].set(jnp.asarray(sizes, jnp.int32))

    sizes = jnp.where(number % 4 == 0, named(packed, number // 4), named(ordinary, number - number // 4 - 1))
    mixed = jax.random.permutation(jax.random.fold_in(own, 3), number_of)
    giver, receiver = mixed[0:number_of // 2 * 2:2], mixed[1:number_of // 2 * 2:2]
    margin = jnp.minimum(sizes[giver] - 1, limit - sizes[receiver]) // 2
    margin = jnp.where((giver == order[0]) | (receiver == order[0]) | (sizes[receiver] == 0), 0, jnp.maximum(margin, 0))
    shifted = jax.random.randint(jax.random.fold_in(own, 4), (number_of // 2,), 0, 1 << 20) % (margin + 1)
    sizes = sizes.at[giver].add(-shifted).at[receiver].add(shifted)
    labels = jnp.searchsorted(jnp.cumsum(sizes), jnp.arange(rows * top), side="right").astype(jnp.int32)
    listing = labels.reshape(top, rows).T
    listing = listing[jax.random.permutation(jax.random.fold_in(own, 1), rows)]
    offset_by = jax.random.randint(jax.random.fold_in(own, 2), (rows, 1), 0, top)
    return jnp.take_along_axis(listing, (jnp.arange(top)[None, :] + offset_by) % top, axis=1)


def portions_of(amount, total, reach, slope, full):
    weights = [(1 << 20) // math.isqrt(standing ** slope) + 1 for standing in range(1, amount + 1)]
    largest = reach if full else min(reach, max(-(-total // amount), total * weights[0] // sum(weights)))
    least = 1 if total - largest >= amount - 1 else 0
    holding, surplus = [largest] + [least] * (amount - 1), total - largest - least * (amount - 1)
    while surplus > 0:
        candidates = [i for i in range(1, amount) if holding[i] < largest] or [i for i in range(1, amount) if holding[i] < reach]
        mass, left = sum([weights[i] for i in candidates]), surplus
        for i in candidates:
            addition = min(reach - holding[i], max(1, left * weights[i] // mass), surplus)
            holding[i] = holding[i] + addition
            surplus = surplus - addition
    return np.array(holding)


def gaussian(rng, dims, width, most, shards=(), kind=jnp.bfloat16):
    gain = level_of(rng, dims, shards, -0.22, 0.18) if shards else 1.0
    array = jax.random.normal(rng, dims, jnp.float32) * width * gain
    return jnp.minimum(jnp.maximum(array, -most), most).astype(kind)


def setup_inputs(seed: int = 0) -> dict:
    seeds = jax.random.split(jax.random.key(seed), 9)
    tokens = gaussian(seeds[0], (TOKENS, D), 1.0, 6.0, ((0, 32), (1, 8)))
    tangent = gaussian(seeds[1], (TOKENS, D), 1.0, 6.0, ((0, 32), (1, 8)))
    cotangent = gaussian(seeds[2], (TOKENS, D), 0.5, 3.0, ((0, 32), (1, 8)))
    routing_keys = jax.random.split(jax.random.fold_in(seeds[3], 1), TOKENS // TOK_DEV)
    routing_turns = jax.random.permutation(jax.random.fold_in(seeds[3], 3), TOKENS // TOK_DEV)
    routing = jax.vmap(lambda own, number: assign_block(jax.random.fold_in(seeds[3], 2), own, number, TOK_DEV, EXPERTS, TOP, CAP, 2))(routing_keys, routing_turns).reshape((TOKENS, TOP))
    gate_weights = jnp.clip(0.1 + 0.5 * jax.random.uniform(seeds[4], (TOKENS, TOP), jnp.float32) ** level_of(seeds[4], (TOKENS, TOP), ((0, 32),), -0.2, 0.2), 0.1, 0.6)
    gate_proj = gaussian(seeds[5], (EXPERTS, D, H), D ** -0.5, 0.0625, ((0, 32), (1, 8)))
    up_proj = gaussian(seeds[6], (EXPERTS, D, H), D ** -0.5, 0.0625, ((0, 32), (1, 8)))
    down_proj = gaussian(seeds[7], (EXPERTS, H, D), H ** -0.5, 0.125, ((0, 32), (2, 8)))
    return dict(tokens=tokens, tangent=tangent, cotangent=cotangent, routing=routing, gate_weights=gate_weights, gate_proj=gate_proj, up_proj=up_proj, down_proj=down_proj)


def second_order(pre_gate, pre_up, tangent_gate, tangent_up, back_hidden):
    sigma = jax.nn.sigmoid(pre_gate)
    first_slope = sigma * (1.0 + pre_gate * (1.0 - sigma))
    second_slope = sigma * (1.0 - sigma) * (2.0 + pre_gate * (1.0 - 2.0 * sigma))
    factor_a = back_hidden * (second_slope * tangent_gate * pre_up + first_slope * tangent_up)
    factor_b = back_hidden * first_slope * tangent_gate
    return factor_a.astype(jnp.bfloat16), factor_b.astype(jnp.bfloat16)


def reference(tokens, tangent, cotangent, routing, gate_weights, gate_proj, up_proj, down_proj):
    routed_flat = routing.reshape(N_EXPERT, TOK_DEV * TOP)
    route_hits = (routed_flat[:, :, None] == jnp.arange(EXPERTS, dtype=jnp.int32)[None, None, :]).astype(jnp.int32)
    slot_index = jnp.sum((jnp.cumsum(route_hits, axis=1) - route_hits) * route_hits, axis=2).astype(jnp.int32)
    source_block = jnp.arange(N_EXPERT, dtype=jnp.int32)[:, None]
    pair_index = jnp.arange(TOK_DEV * TOP, dtype=jnp.int32)[None, :]
    token_index = (source_block * TOK_DEV + pair_index // TOP).astype(jnp.int32)
    row_index = (source_block * CAP + slot_index).astype(jnp.int32)
    token_table = jnp.zeros((EXPERTS, N_EXPERT * CAP), jnp.int32).at[routed_flat, row_index].set(token_index)
    weight_table = jnp.zeros((EXPERTS, N_EXPERT * CAP), jnp.float32).at[routed_flat, row_index].set(
        gate_weights.reshape(N_EXPERT, TOK_DEV * TOP).astype(jnp.float32))

    def per_expert(carry, expert_id):
        picked = token_table[expert_id]
        row_weight = weight_table[expert_id]
        x_rows = tokens[picked]
        v_rows = tangent[picked]
        c_rows = cotangent[picked]
        gate_matrix = gate_proj[expert_id]
        up_matrix = up_proj[expert_id]
        down_matrix = down_proj[expert_id]
        pre_gate = jnp.dot(x_rows, gate_matrix, preferred_element_type=jnp.float32)
        pre_up = jnp.dot(x_rows, up_matrix, preferred_element_type=jnp.float32)
        tangent_gate = jnp.dot(v_rows, gate_matrix, preferred_element_type=jnp.float32)
        tangent_up = jnp.dot(v_rows, up_matrix, preferred_element_type=jnp.float32)
        back_hidden = jnp.dot(c_rows, down_matrix.T, preferred_element_type=jnp.float32)
        factor_a, factor_b = second_order(pre_gate, pre_up, tangent_gate, tangent_up, back_hidden)
        rows_out = (jnp.dot(factor_a, gate_matrix.T, preferred_element_type=jnp.float32)
                    + jnp.dot(factor_b, up_matrix.T, preferred_element_type=jnp.float32)).astype(jnp.bfloat16)
        carry = carry.at[picked].add(row_weight[:, None] * rows_out.astype(jnp.float32))
        return carry, None

    start_value = jnp.zeros((TOKENS, D), jnp.float32)
    result, unused = lax.scan(per_expert, start_value, jnp.arange(EXPERTS, dtype=jnp.int32))
    return result
```

```python
import jax
import jax.numpy as jnp
from jax import lax
from jax.experimental import pallas as pl
from jax.experimental.pallas import tpu as pltpu
from jax.sharding import PartitionSpec as P

MESH = pl.DeviceIdType.MESH
BF16 = jnp.bfloat16
F32 = jnp.float32

TOP = 8
TOK = 64
CAP = 18
DC = 896
H = 2048
NZ = 8
CH = H // NZ
NG = 4
SRC = 8
GR = SRC * CAP
SUMS = 5
MR = SUMS * GR + 16
BR = 3 * TOK + 16
PAD = 32


def nt(a, b):
    return lax.dot_general(a, b, (((1,), (1,)), ((), ())), preferred_element_type=F32)


def nn(a, b):
    return jnp.dot(a, b, preferred_element_type=F32)


def kernel(
    x_ref, v_ref, c_ref, rt_ref, routing_ref, gw_ref, gate_ref, up_ref, down_ref, out_ref,
    gate_v, up_v, down_v, tok, xrows, part, rs_s, rs_r, fac, acc, sbuf, rbuf, wmat,
    w_sem, l_sem, y_ss, y_rs, x_ss, x_rs, x3_ss, x3_rs, sib_ss, sib_rs,
    rs_ss, rs_rs, ag_ss, ag_rs, rt_ss, rt_rs,
):
    me = lax.axis_index("dp")
    ex = lax.axis_index("expert")
    px = ex // 8
    py = (ex // 2) % 4
    pc = ex % 2

    def at_xy(dx, dy, dc):
        return (me, (((px + dx) % 4) * 4 + (py + dy) % 4) * 2 + (pc + dc) % 2)

    z_dev = ((me + NZ - 1) % NZ, ex), ((me + 1) % NZ, ex)
    y_dev = at_xy(0, 1, 0), at_xy(0, 3, 0)
    x_dev = at_xy(1, 0, 0), at_xy(3, 0, 0)
    sib_dev = at_xy(0, 0, 1)

    def remote(src, dst, ss, rs, dev):
        return pltpu.make_async_remote_copy(
            src_ref=src, dst_ref=dst, send_sem=ss, recv_sem=rs, device_id=dev, device_id_type=MESH
        )

    loads = [
        pltpu.make_async_copy(x_ref, tok.at[0, 0, 0, pl.ds(0, TOK)], l_sem.at[0]),
        pltpu.make_async_copy(v_ref, tok.at[0, 0, 0, pl.ds(TOK, TOK)], l_sem.at[1]),
        pltpu.make_async_copy(c_ref, tok.at[0, 0, 0, pl.ds(2 * TOK, TOK)], l_sem.at[2]),
        pltpu.make_async_copy(rt_ref, tok.at[0, 0, 0, pl.ds(3 * TOK, 16)], l_sem.at[3]),
    ]
    weights = [
        pltpu.make_async_copy(gate_ref, gate_v, w_sem.at[0]),
        pltpu.make_async_copy(up_ref, up_v, w_sem.at[1]),
        pltpu.make_async_copy(down_ref, down_v, w_sem.at[2]),
    ]
    for cp in loads:
        cp.start()
    for cp in weights:
        cp.start()

    bar = pltpu.get_barrier_semaphore()
    for d in (0, 1):
        pl.semaphore_signal(bar, 1, device_id=z_dev[d], device_id_type=MESH)

    def greet(o, _):
        pl.semaphore_signal(bar, 1, device_id=(me, (ex + o) % 32), device_id_type=MESH)
        return 0

    lax.fori_loop(1, 32, greet, 0)
    pl.semaphore_wait(bar, 33)

    def y_copy(i):
        if i == 0:
            return remote(tok.at[0, 0, 0], tok.at[0, 0, 3], y_ss.at[0], y_rs.at[0], y_dev[0])
        if i == 1:
            return remote(tok.at[0, 0, 0], tok.at[0, 0, 1], y_ss.at[1], y_rs.at[1], y_dev[1])
        if i == 2:
            rows = pl.ds(0, 96)
            return remote(tok.at[0, 0, 3, rows], tok.at[0, 0, 2, rows], y_ss.at[2], y_rs.at[2], y_dev[0])
        rows = pl.ds(96, BR - 96)
        return remote(tok.at[0, 0, 1, rows], tok.at[0, 0, 2, rows], y_ss.at[3], y_rs.at[3], y_dev[1])

    def x_copy(d, dy):
        return remote(
            tok.at[0, 0, dy], tok.at[2 - d, 0, dy], x_ss.at[d * 4 + dy], x_rs.at[d * 4 + dy], x_dev[d]
        )

    def x3_copy(dy):
        g, d = (1, 1) if dy < 2 else (2, 0)
        return remote(tok.at[g, 0, dy], tok.at[3, 0, dy], x3_ss.at[dy], x3_rs.at[dy], x_dev[d])

    def sib_copy(g, dy):
        return remote(
            tok.at[g, 0, dy], tok.at[g, 1, dy], sib_ss.at[g * 4 + dy], sib_rs.at[g * 4 + dy], sib_dev
        )

    def rs_copy(g, d, k, h):
        s = (((g % 2) * 2 + d) * 4 + k) * 2 + h
        r = ((g * 2 + d) * 4 + k) * 2 + h
        return remote(rs_s.at[s], rs_r.at[r], rs_ss.at[s], rs_rs.at[r], z_dev[d])

    def ag_copy(g, d, k, h):
        i = ((g * 2 + d) * 4 + k) * 2 + h
        src, dst = (k, k + 1) if d == 0 else ((8 - k) % 8, 7 - k)
        return remote(
            fac.at[(g * 8 + src) * 2 + h], fac.at[(g * 8 + dst) * 2 + h], ag_ss.at[i], ag_rs.at[i], z_dev[d]
        )

    def dx_of(g):
        return g + g // 2 - 2 * (g // 3)

    def back_copy(g, j):
        dev = at_xy(dx_of(g), j % 4, j // 4)
        return remote(sbuf.at[g * SRC + j], rbuf.at[ex], rt_ss.at[g * SRC + j], rt_rs.at[ex], dev)

    def gather(g):
        lane = lax.broadcasted_iota(jnp.int32, (8, 128), 1)
        tri_r = lax.broadcasted_iota(jnp.int32, (128, 128), 0)
        tri_c = lax.broadcasted_iota(jnp.int32, (128, 128), 1)
        tri = ((tri_r < tri_c) & (tri_r // 64 == tri_c // 64)).astype(F32).astype(BF16)
        row = lax.broadcasted_iota(jnp.int32, (GR, 128), 0).astype(F32)
        low = lax.broadcasted_iota(jnp.int32, (16, 128), 1) < 64
        exf = ex.astype(F32)
        hots = []
        for c in range(2):
            for p in range(2):
                ra = tok[g, c, 2 * p, pl.ds(3 * TOK, 16), pl.ds(0, 128)].astype(F32)
                rb = tok[g, c, 2 * p + 1, pl.ds(3 * TOK, 16), pl.ds(0, 128)].astype(F32)
                hit = jnp.where(jnp.where(low, ra, rb) == exf, 1.0, 0.0)
                hit = jnp.broadcast_to(jnp.sum(hit, axis=0, keepdims=True), (8, 128))
                rank = nn(hit.astype(BF16), tri)
                first = (CAP * (4 * c + 2 * p) + CAP * (lane // 64)).astype(F32)
                target = jnp.where(hit > 0.5, rank + first, -1.0)
                hots.append(jnp.where(row == target[0:1], 1.0, 0.0).astype(BF16))
        hot = jnp.concatenate(hots, axis=1)
        for a in range(3):
            rows = jnp.concatenate(
                [tok[g, c, y, pl.ds(a * TOK, TOK), :] for c in range(2) for y in range(4)], axis=0
            )
            xrows[g % 2, pl.ds(a * GR, GR), :] = nn(hot, rows).astype(BF16)

    def products(g, d, chunk):
        first = pl.multiple_of(chunk * CH, CH)
        cols = pl.ds(first, CH)
        xv = xrows[g % 2, pl.ds(0, 2 * GR), :]
        part[d, pl.ds(0, 2 * GR), :] = nn(xv, gate_v[:, cols])
        part[d, pl.ds(2 * GR, 2 * GR), :] = nn(xv, up_v[:, cols])
        part[d, pl.ds(4 * GR, GR), :] = nt(xrows[g % 2, pl.ds(2 * GR, GR), :], down_v[cols, :])

    def scales(r):
        return jnp.exp2(rs_r[r, pl.ds(SUMS * GR, 16), :].astype(F32) * (1.0 / 256.0))

    def send_sums(g, d, k, h, came):
        s = (((g % 2) * 2 + d) * 4 + k) * 2 + h
        own = 0 if k == 0 else d

        @pl.when(g >= 2)
        def _():
            rs_copy(g, d, k, h).wait_send()

        r = ((g * 2 + d) * 4 + k - 1) * 2 + h
        if came:
            rs_copy(g, d, k - 1, h).wait_recv()
            sc = scales(r)
        codes = jnp.zeros((16, 128), F32)
        at = lax.broadcasted_iota(jnp.int32, (16, 128), 0)
        for p in range(SUMS):
            rows = pl.ds(p * GR, GR)
            blk = part[own, rows, pl.ds(h * 128, 128)]
            if came:
                blk = blk + rs_r[r, rows, :].astype(F32) * sc[p : p + 1]
            most = jnp.max(jnp.abs(blk), axis=0, keepdims=True)
            code = jnp.ceil(256.0 * jnp.log2(jnp.maximum(most, 1e-30) * (1.0 / 32760.0)))
            inv = jnp.exp2(code * (-1.0 / 256.0))
            rs_s[s, rows, :] = jnp.round(blk * inv).astype(jnp.int32).astype(jnp.int16)
            codes = jnp.where(at == p, code, codes)
        rs_s[s, pl.ds(SUMS * GR, 16), :] = codes.astype(jnp.int32).astype(jnp.int16)
        rs_copy(g, d, k, h).start()

    def stage_0(g):
        products(g, 0, (me + 4) % NZ)
        for d in (0, 1):
            send_sums(g, d, 0, d, False)

    def stage(g, k):
        products(g, 0, (me + NZ - (4 - k)) % NZ)
        products(g, 1, (me + 4 - k) % NZ)
        if k == 1:
            send_sums(g, 0, 1, 1, False)
            send_sums(g, 1, 1, 0, False)
            send_sums(g, 0, 1, 0, True)
            send_sums(g, 1, 1, 1, True)
        else:
            for h in (1, 0):
                for d in (0, 1):
                    send_sums(g, d, k, h if d == 0 else 1 - h, True)

    def stage_4(g):
        products(g, 0, me)
        for h in (0, 1):
            total = []
            r = [((g * 2 + d) * 4 + 3) * 2 + h for d in (0, 1)]
            for d in (0, 1):
                rs_copy(g, d, 3, h).wait_recv()
            sc = [scales(r[0]), scales(r[1])]
            for p in range(SUMS):
                rows = pl.ds(p * GR, GR)
                blk = part[0, rows, pl.ds(h * 128, 128)]
                for d in (0, 1):
                    blk = blk + rs_r[r[d], rows, :].astype(F32) * sc[d][p : p + 1]
                total.append(blk)
            a, da, b, db, dh = total
            sig = 1.0 / (1.0 + jnp.exp(-a))
            s1 = sig * (1.0 + a * (1.0 - sig))
            s2 = sig * (1.0 - sig) * (2.0 + a * (1.0 - 2.0 * sig))
            fac[g * 16 + h, pl.ds(0, GR), :] = (dh * (s2 * da * b + s1 * db)).astype(BF16)
            fac[g * 16 + h, pl.ds(GR, GR), :] = (dh * s1 * da).astype(BF16)
            for d in (0, 1):
                ag_copy(g, d, 0, h).start()

    def add_rows(g, r, new):
        cols = pl.ds(pl.multiple_of(((me + r) % NZ) * CH, CH), CH)
        f = jnp.concatenate([fac[(g * 8 + r) * 2], fac[(g * 8 + r) * 2 + 1]], axis=1)
        more = nt(f[0:GR], gate_v[:, cols]) + nt(f[GR:], up_v[:, cols])
        acc[...] = more if new else acc[...] + more

    def gather_stage(g, k):
        for h in (0, 1):
            for d in (0, 1):
                ag_copy(g, d, k - 1, h).wait_recv()
                if k < 3 or h == d:
                    ag_copy(g, d, k, h).start()
        if k == 1:
            add_rows(g, 0, True)
        add_rows(g, k, False)
        add_rows(g, 8 - k, False)

    def last_stage(g):
        ag_copy(g, 0, 3, 0).wait_recv()
        ag_copy(g, 1, 3, 1).wait_recv()
        add_rows(g, 4, False)
        rows = acc[...].astype(BF16)
        o = lax.broadcasted_iota(jnp.int32, (SRC * PAD, GR), 0)
        i = lax.broadcasted_iota(jnp.int32, (SRC * PAD, GR), 1)
        hot = jnp.where((o % PAD < CAP) & (i == (o // PAD) * CAP + o % PAD), 1.0, 0.0).astype(BF16)
        spread = nn(hot, rows).astype(BF16)
        for j in range(SRC):
            sbuf[g * SRC + j] = spread[j * PAD : (j + 1) * PAD]
        for j in range(SRC):
            if j == 0:

                @pl.when(g == 0)
                def _():
                    pltpu.make_async_copy(sbuf.at[0], rbuf.at[ex], rt_rs.at[ex]).start()

                @pl.when(g > 0)
                def _():
                    back_copy(g, 0).start()
            else:
                back_copy(g, j).start()

    for cp in loads:
        cp.wait()
    y_copy(0).start()
    y_copy(1).start()
    sib_copy(0, 0).start()
    x_copy(0, 0).start()
    x_copy(1, 0).start()

    hits = jnp.zeros((TOK, 128), F32)
    lane = lax.broadcasted_iota(jnp.int32, (TOK, 128), 1)
    for k in range(TOP):
        hits = hits + jnp.where(routing_ref[:, k : k + 1] == lane, 1.0, 0.0)
    tri = lax.broadcasted_iota(jnp.int32, (TOK, TOK), 1) < lax.broadcasted_iota(jnp.int32, (TOK, TOK), 0)
    place = nn(jnp.where(tri, 1.0, 0.0).astype(BF16), hits.astype(BF16)) + (lane * PAD).astype(F32)
    col = lax.broadcasted_iota(jnp.int32, (TOK, 32 * PAD), 1).astype(F32)
    w = jnp.zeros((TOK, 32 * PAD), F32)
    for k in range(TOP):
        at = jnp.sum(jnp.where(routing_ref[:, k : k + 1] == lane, place, 0.0), axis=1, keepdims=True)
        w = w + jnp.where(col == at, gw_ref[:, k : k + 1], 0.0)
    for i in range(3):
        piece = w.astype(BF16)
        wmat[pl.ds(i * TOK, TOK), :] = piece
        w = w - piece.astype(F32)

    y_copy(1).wait_recv()
    y_copy(3).start()
    y_copy(0).wait_recv()
    y_copy(2).start()
    for dy in (1, 3):
        sib_copy(0, dy).start()
        x_copy(0, dy).start()
        x_copy(1, dy).start()
    y_copy(2).wait_recv()
    y_copy(3).wait_recv()
    sib_copy(0, 2).start()
    x_copy(0, 2).start()
    x_copy(1, 2).start()
    for cp in weights:
        cp.wait()
    for dy in (0, 1, 3, 2):
        sib_copy(0, dy).wait_recv()
    gather(0)
    stage_0(0)

    def turn(i, _):
        for k in (1, 2, 3):

            @pl.when(i < NG)
            def _():
                stage(i, k)

            @pl.when(i >= 1)
            def _():
                gather_stage(i - 1, k)

        @pl.when(i == 0)
        def _():
            for dy in range(4):
                for d in (1, 0):
                    x_copy(d, dy).wait_recv()
                    sib_copy(2 - d, dy).start()
            for dy in range(4):
                x3_copy(dy).start()
            for dy in range(4):
                sib_copy(1, dy).wait_recv()

        @pl.when(i == 1)
        def _():
            for dy in range(4):
                x3_copy(dy).wait_recv()
                sib_copy(3, dy).start()
            for dy in range(4):
                sib_copy(2, dy).wait_recv()

        @pl.when(i == 2)
        def _():
            for dy in range(4):
                sib_copy(3, dy).wait_recv()

        @pl.when(i < NG - 1)
        def _():
            gather(i + 1)
            stage_0(i + 1)

        @pl.when(i >= 1)
        def _():
            last_stage(i - 1)

        @pl.when(i < NG)
        def _():
            stage_4(i)

        return 0

    lax.fori_loop(0, NG + 1, turn, 0)

    def arrive(e, _):
        pltpu.make_async_copy(rbuf.at[e], rbuf.at[e], rt_rs.at[e]).wait()
        return 0

    lax.fori_loop(0, 32, arrive, 0)
    parts = nn(wmat[...], jnp.concatenate([rbuf[e] for e in range(32)], axis=0))
    out_ref[...] = parts[2 * TOK :] + parts[TOK : 2 * TOK] + parts[:TOK]

    for i in range(4):
        y_copy(i).wait_send()
        x3_copy(i).wait_send()
        for d in (0, 1):
            x_copy(d, i).wait_send()
        for g in range(NG):
            sib_copy(g, i).wait_send()

    def left(g, _):
        for d in (0, 1):
            for k in range(4):
                for h in (0, 1):
                    if k > 0 or h == d:

                        @pl.when(g >= 2)
                        def _():
                            rs_copy(g, d, k, h).wait_send()

                    if k < 3 or h == d:
                        ag_copy(g, d, k, h).wait_send()
        for j in range(SRC):
            if j == 0:

                @pl.when(g > 0)
                def _():
                    back_copy(g, 0).wait_send()
            else:
                back_copy(g, j).wait_send()
        return 0

    lax.fori_loop(0, NG, left, 0)


def shards(tokens, tangent, cotangent, routing, gate_weights, gate_proj, up_proj, down_proj):
    names = routing.T.astype(BF16)
    names = jnp.concatenate([names, names], axis=1)
    names = jnp.pad(names, ((0, 8), (0, DC - 128)), constant_values=-1.0)
    dma = pltpu.SemaphoreType.DMA
    anywhere = pl.BlockSpec(memory_space=pl.ANY)
    vmem = pl.BlockSpec(memory_space=pltpu.VMEM)
    return pl.pallas_call(
        kernel,
        out_shape=jax.ShapeDtypeStruct((TOK, DC), F32),
        in_specs=[anywhere] * 4 + [vmem] * 2 + [anywhere] * 3,
        out_specs=vmem,
        scratch_shapes=[
            pltpu.VMEM((DC, H), BF16),
            pltpu.VMEM((DC, H), BF16),
            pltpu.VMEM((H, DC), BF16),
            pltpu.VMEM((NG, 2, 4, BR, DC), BF16),
            pltpu.VMEM((2, 3 * GR, DC), BF16),
            pltpu.VMEM((2, SUMS * GR, CH), F32),
            pltpu.VMEM((32, MR, 128), jnp.int16),
            pltpu.VMEM((64, MR, 128), jnp.int16),
            pltpu.VMEM((NG * 16, 2 * GR, 128), BF16),
            pltpu.VMEM((GR, DC), F32),
            pltpu.VMEM((NG * SRC, PAD, DC), BF16),
            pltpu.VMEM((32, PAD, DC), BF16),
            pltpu.VMEM((3 * TOK, 32 * PAD), BF16),
            dma((3,)), dma((4,)), dma((4,)), dma((4,)), dma((8,)), dma((8,)), dma((4,)), dma((4,)),
            dma((16,)), dma((16,)), dma((32,)), dma((64,)), dma((64,)), dma((64,)), dma((32,)), dma((32,)),
        ],
        compiler_params=pltpu.CompilerParams(
            collective_id=0, has_side_effects=True, vmem_limit_bytes=61 * 1024 * 1024
        ),
        cost_estimate=pl.CostEstimate(
            flops=2 * 7 * 576 * DC * H, bytes_accessed=12_000_000, transcendentals=576 * H // NZ
        ),
    )(tokens, tangent, cotangent, names, routing, gate_weights, gate_proj[0], up_proj[0], down_proj[0])


def solution(mesh):
    in_specs = (
        P("expert", "dp"),
        P("expert", "dp"),
        P("expert", "dp"),
        P("expert", None),
        P("expert", None),
        P("expert", "dp", None),
        P("expert", "dp", None),
        P("expert", None, "dp"),
    )
    return jax.shard_map(
        shards, mesh=mesh, in_specs=in_specs, out_specs=P("expert", "dp"), check_vma=False
    )
```

```python
import jax
import jax.numpy as jnp
from jax import lax
from jax.experimental import pallas as pl
from jax.experimental.pallas import tpu as pltpu
from jax.sharding import PartitionSpec as P

MESH = pl.DeviceIdType.MESH
BF16 = jnp.bfloat16
F32 = jnp.float32

TOP = 8
TOK = 64
CAP = 18
DC = 896
H = 2048
NZ = 8
CH = H // NZ
NG = 4
SRC = 8
GR = SRC * CAP
SUMS = 5
CHIPS = (
    ((0, 0), (0, 1), (1, 0), (0, 3)),
    ((3, 0), (0, 2), (2, 0), (3, 2)),
    ((1, 2), (2, 1), (2, 3), (2, 2)),
    ((1, 1), (1, 3), (3, 1), (3, 3)),
)
MR = SUMS * GR + 16
BR = 16 + 3 * TOK
PARTS = (pl.ds(0, 16 + TOK), pl.ds(16 + TOK, 2 * TOK))
PAD = 32


def nt(a, b):
    return lax.dot_general(a, b, (((1,), (1,)), ((), ())), preferred_element_type=F32)


def nn(a, b):
    return jnp.dot(a, b, preferred_element_type=F32)


def kernel(
    x_ref, v_ref, c_ref, routing_ref, gw_ref, gate_ref, up_ref, down_ref, out_ref,
    gate_v, up_v, down_v, tok, xrows, part, rs_s, rs_r, fac, acc, sbuf, rbuf, wmat,
    w_sem, l_sem, y_ss, y_rs, x_ss, x_rs, x3_ss, x3_rs, sib_ss, sib_rs,
    rs_ss, rs_rs, ag_ss, ag_rs, rt_ss, rt_rs,
):
    me = lax.axis_index("dp")
    ex = lax.axis_index("expert")
    px = ex // 8
    py = (ex // 2) % 4
    pc = ex % 2

    def at_xy(dx, dy, dc):
        return (me, (((px + dx + 4) % 4) * 4 + (py + dy + 4) % 4) * 2 + (pc + dc) % 2)

    z_dev = ((me + NZ - 1) % NZ, ex), ((me + 1) % NZ, ex)
    y_dev = at_xy(0, 1, 0), at_xy(0, 3, 0)
    x_dev = at_xy(1, 0, 0), at_xy(3, 0, 0)
    sib_dev = at_xy(0, 0, 1)

    def remote(src, dst, ss, rs, dev):
        return pltpu.make_async_remote_copy(
            src_ref=src, dst_ref=dst, send_sem=ss, recv_sem=rs, device_id=dev, device_id_type=MESH
        )

    loads = [
        pltpu.make_async_copy(x_ref, tok.at[0, 0, 0, pl.ds(16, TOK)], l_sem.at[0]),
        pltpu.make_async_copy(v_ref, tok.at[0, 0, 0, pl.ds(16 + TOK, TOK)], l_sem.at[1]),
        pltpu.make_async_copy(c_ref, tok.at[0, 0, 0, pl.ds(16 + 2 * TOK, TOK)], l_sem.at[2]),
    ]
    weights = [
        pltpu.make_async_copy(gate_ref, gate_v, w_sem.at[0]),
        pltpu.make_async_copy(up_ref, up_v, w_sem.at[1]),
        pltpu.make_async_copy(down_ref, down_v, w_sem.at[2]),
    ]
    for cp in loads:
        cp.start()
    for cp in weights:
        cp.start()

    bar = pltpu.get_barrier_semaphore()
    for d in (0, 1):
        pl.semaphore_signal(bar, 1, device_id=z_dev[d], device_id_type=MESH)

    def greet(o, _):
        pl.semaphore_signal(bar, 1, device_id=(me, (ex + o) % 32), device_id_type=MESH)
        return 0

    lax.fori_loop(1, 32, greet, 0)

    named = jnp.concatenate([routing_ref[...].astype(F32), jnp.full((8, TOK), -1.0, F32)], axis=0).astype(BF16)
    twice = lax.broadcasted_iota(jnp.int32, (TOK, 128), 1) % TOK == lax.broadcasted_iota(jnp.int32, (TOK, 128), 0)
    tok[0, 0, 0, pl.ds(0, 16), :] = jnp.zeros((16, DC), BF16)
    tok[0, 0, 0, pl.ds(0, 16), pl.ds(0, 128)] = nn(named, jnp.where(twice, 1.0, 0.0).astype(BF16)).astype(BF16)
    pl.semaphore_wait(bar, 33)

    def slot(col, dy):
        return next((g, i) for g in range(NG) for i in range(4) if CHIPS[g][i] == (col, dy))

    def block(col, dy, q=None):
        g, i = slot(col, dy)
        if q is None:
            return tok.at[g, 0, i]
        return tok.at[g, 0, i, PARTS[q]]

    def y_copy(i, q):
        if i == 0:
            return remote(block(0, 0, q), block(0, 3, q), y_ss.at[q], y_rs.at[q], y_dev[0])
        if i == 1:
            return remote(block(0, 0, q), block(0, 1, q), y_ss.at[2 + q], y_rs.at[2 + q], y_dev[1])
        src = block(0, 3, q) if q == 0 else block(0, 1, q)
        return remote(src, block(0, 2, q), y_ss.at[4 + q], y_rs.at[4 + q], y_dev[q])

    def x_copy(d, dy, q=None):
        i = d * 5 + (dy if dy else 4 * (q or 0))
        return remote(block(0, dy, q), block(1 if d else 3, dy, q), x_ss.at[i], x_rs.at[i], x_dev[d])

    def x3_copy(dy):
        col, d = (1, 1) if dy < 2 else (3, 0)
        return remote(block(col, dy), block(2, dy), x3_ss.at[dy], x3_rs.at[dy], x_dev[d])

    def sib_copy(g, i, q=None):
        n = g * 4 + i + (16 if q == 1 else 0)
        rows = pl.ds(0, BR) if q is None else PARTS[q]
        return remote(tok.at[g, 0, i, rows], tok.at[g, 1, i, rows], sib_ss.at[n], sib_rs.at[n], sib_dev)

    def rs_copy(g, d, k, h):
        s = (((g % 2) * 2 + d) * 4 + k) * 2 + h
        r = ((g * 2 + d) * 4 + k) * 2 + h
        return remote(rs_s.at[s], rs_r.at[r], rs_ss.at[s], rs_rs.at[r], z_dev[d])

    def ag_copy(g, d, k, h, q):
        i = (((g * 2 + d) * 4 + k) * 2 + h) * 2 + q
        src, dst = (k, k + 1) if d == 0 else ((8 - k) % 8, 7 - k)
        rows = pl.ds(q * GR, GR)
        return remote(
            fac.at[(g * 8 + src) * 2 + h, rows], fac.at[(g * 8 + dst) * 2 + h, rows], ag_ss.at[i], ag_rs.at[i], z_dev[d]
        )

    def back_copy(g, j):
        dx, dy = CHIPS[g][j % 4]
        n = g * SRC + j
        return remote(sbuf.at[n], rbuf.at[n], rt_ss.at[n], rt_rs.at[n], at_xy(dx, dy, j // 4))

    def gather(g):
        lane = lax.broadcasted_iota(jnp.int32, (8, 128), 1)
        tri_r = lax.broadcasted_iota(jnp.int32, (128, 128), 0)
        tri_c = lax.broadcasted_iota(jnp.int32, (128, 128), 1)
        tri = ((tri_r < tri_c) & (tri_r // 64 == tri_c // 64)).astype(F32).astype(BF16)
        row = lax.broadcasted_iota(jnp.int32, (GR, 128), 0).astype(F32)
        low = lax.broadcasted_iota(jnp.int32, (16, 128), 1) < 64
        exf = ex.astype(F32)
        hots = []
        for c in range(2):
            for p in range(2):
                ra = tok[g, c, 2 * p, pl.ds(0, 16), pl.ds(0, 128)].astype(F32)
                rb = tok[g, c, 2 * p + 1, pl.ds(0, 16), pl.ds(0, 128)].astype(F32)
                hit = jnp.where(jnp.where(low, ra, rb) == exf, 1.0, 0.0)
                hit = jnp.broadcast_to(jnp.sum(hit, axis=0, keepdims=True), (8, 128))
                rank = nn(hit.astype(BF16), tri)
                first = (CAP * (4 * c + 2 * p) + CAP * (lane // 64)).astype(F32)
                target = jnp.where(hit > 0.5, rank + first, -1.0)
                hots.append(jnp.where(row == target[0:1], 1.0, 0.0).astype(BF16))
        hot = jnp.concatenate(hots, axis=1)
        for a in range(3):
            rows = jnp.concatenate(
                [tok[g, c, y, pl.ds(16 + a * TOK, TOK), :] for c in range(2) for y in range(4)], axis=0
            )
            xrows[g % 2, pl.ds(a * GR, GR), :] = nn(hot, rows).astype(BF16)

    def products(g, d, chunk):
        first = pl.multiple_of(chunk * CH, CH)
        cols = pl.ds(first, CH)
        xv = xrows[g % 2, pl.ds(0, 2 * GR), :]
        part[d, pl.ds(0, 2 * GR), :] = nn(xv, gate_v[:, cols])
        part[d, pl.ds(2 * GR, 2 * GR), :] = nn(xv, up_v[:, cols])
        part[d, pl.ds(4 * GR, GR), :] = nt(xrows[g % 2, pl.ds(2 * GR, GR), :], down_v[cols, :])

    def scales(r):
        return jnp.exp2(rs_r[r, pl.ds(SUMS * GR, 16), :].astype(F32) * (1.0 / 256.0))

    def send_sums(g, d, k, h, came):
        s = (((g % 2) * 2 + d) * 4 + k) * 2 + h
        own = 2 if k == 0 else 3 + d if k == 1 else d

        @pl.when(g >= 2)
        def _():
            rs_copy(g, d, k, h).wait_send()

        r = ((g * 2 + d) * 4 + k - 1) * 2 + h
        if came:
            rs_copy(g, d, k - 1, h).wait_recv()
            sc = scales(r)
        codes = jnp.zeros((16, 128), F32)
        at = lax.broadcasted_iota(jnp.int32, (16, 128), 0)
        for p in range(SUMS):
            rows = pl.ds(p * GR, GR)
            blk = part[own, rows, pl.ds(h * 128, 128)]
            if came:
                blk = blk + rs_r[r, rows, :].astype(F32) * sc[p : p + 1]
            most = jnp.max(jnp.abs(blk), axis=0, keepdims=True)
            code = jnp.ceil(256.0 * jnp.log2(jnp.maximum(most, 1e-30) * (1.0 / 32760.0)))
            inv = jnp.exp2(code * (-1.0 / 256.0))
            rs_s[s, rows, :] = jnp.round(blk * inv).astype(jnp.int32).astype(jnp.int16)
            codes = jnp.where(at == p, code, codes)
        rs_s[s, pl.ds(SUMS * GR, 16), :] = codes.astype(jnp.int32).astype(jnp.int16)
        rs_copy(g, d, k, h).start()

    def stage_0(g):
        products(g, 2, (me + 4) % NZ)
        for d in (0, 1):
            send_sums(g, d, 0, d, False)
        products(g, 3, (me + NZ - 3) % NZ)
        products(g, 4, (me + 3) % NZ)
        for d in (0, 1):
            send_sums(g, d, 1, 1 - d, False)

    def stage(g, k):
        if k == 1:
            for d in (0, 1):
                send_sums(g, d, 1, d, True)
            return
        products(g, 0, (me + NZ - (4 - k)) % NZ)
        products(g, 1, (me + 4 - k) % NZ)
        for h in (1, 0):
            for d in (0, 1):
                send_sums(g, d, k, h if d == 0 else 1 - h, True)

    def stage_4(g):
        products(g, 2, me)
        for h in (0, 1):
            total = []
            r = [((g * 2 + d) * 4 + 3) * 2 + h for d in (0, 1)]
            for d in (0, 1):
                rs_copy(g, d, 3, h).wait_recv()
            sc = [scales(r[0]), scales(r[1])]
            for p in range(SUMS):
                rows = pl.ds(p * GR, GR)
                blk = part[2, rows, pl.ds(h * 128, 128)]
                for d in (0, 1):
                    blk = blk + rs_r[r[d], rows, :].astype(F32) * sc[d][p : p + 1]
                total.append(blk)
            a, da, b, db, dh = total
            sig = 1.0 / (1.0 + jnp.exp(-a))
            s1 = sig * (1.0 + a * (1.0 - sig))
            s2 = sig * (1.0 - sig) * (2.0 + a * (1.0 - 2.0 * sig))
            fac[g * 16 + h, pl.ds(0, GR), :] = (dh * (s2 * da * b + s1 * db)).astype(BF16)
            fac[g * 16 + h, pl.ds(GR, GR), :] = (dh * s1 * da).astype(BF16)
            for q in (0, 1):
                for d in (0, 1):
                    ag_copy(g, d, 0, h, q).start()

    def add_rows(g, r, new):
        cols = pl.ds(pl.multiple_of(((me + r) % NZ) * CH, CH), CH)
        f = jnp.concatenate([fac[(g * 8 + r) * 2], fac[(g * 8 + r) * 2 + 1]], axis=1)
        more = nt(f[0:GR], gate_v[:, cols]) + nt(f[GR:], up_v[:, cols])
        acc[...] = more if new else acc[...] + more

    def gather_stage(g, k):
        for h in (0, 1):
            for q in (0, 1):
                for d in (0, 1):
                    ag_copy(g, d, k - 1, h, q).wait_recv()
                    if k < 3 or h == d:
                        ag_copy(g, d, k, h, q).start()
        if k == 1:
            add_rows(g, 0, True)
        add_rows(g, k, False)
        add_rows(g, 8 - k, False)

    def last_stage(g):
        for q in (0, 1):
            for d in (0, 1):
                ag_copy(g, d, 3, d, q).wait_recv()
        add_rows(g, 4, False)
        rows = acc[...].astype(BF16)
        o = lax.broadcasted_iota(jnp.int32, (SRC * PAD, GR), 0)
        i = lax.broadcasted_iota(jnp.int32, (SRC * PAD, GR), 1)
        hot = jnp.where((o % PAD < CAP) & (i == (o // PAD) * CAP + o % PAD), 1.0, 0.0).astype(BF16)
        spread = nn(hot, rows).astype(BF16)
        for j in range(SRC):
            sbuf[g * SRC + j] = spread[j * PAD : (j + 1) * PAD]
        for at in range(NG):

            @pl.when(g == at)
            def _():
                for j in range(SRC):
                    if at == 0 and j == 0:
                        pltpu.make_async_copy(sbuf.at[0], rbuf.at[0], rt_rs.at[0]).start()
                    else:
                        back_copy(at, j).start()

    loads[0].wait()
    for q in (0, 1):
        if q == 1:
            loads[1].wait()
            loads[2].wait()
        y_copy(0, q).start()
        y_copy(1, q).start()
        x_copy(1, 0, q).start()
        sib_copy(0, 0, q).start()
        x_copy(0, 0, q).start()

    same = lax.broadcasted_iota(jnp.int32, (TOK, TOK), 0) == lax.broadcasted_iota(jnp.int32, (TOK, TOK), 1)
    same = jnp.where(same, 1.0, 0.0).astype(BF16)
    names = nt(same, routing_ref[...].astype(F32).astype(BF16))
    rest = gw_ref[...]
    gw = jnp.zeros((TOK, TOP), F32)
    for i in range(3):
        piece = rest.astype(BF16)
        gw = gw + nt(same, piece)
        rest = rest - piece.astype(F32)
    hits = jnp.zeros((TOK, 128), F32)
    lane = lax.broadcasted_iota(jnp.int32, (TOK, 128), 1).astype(F32)
    for k in range(TOP):
        hits = hits + jnp.where(names[:, k : k + 1] == lane, 1.0, 0.0)
    order = jnp.zeros((TOK, 128), F32)
    for n in range(NG * SRC):
        dx, dy = CHIPS[n // SRC][n % 4]
        order = jnp.where(lane == at_xy(-dx, -dy, n % SRC // 4)[1].astype(F32), float(n), order)
    tri = lax.broadcasted_iota(jnp.int32, (TOK, TOK), 1) < lax.broadcasted_iota(jnp.int32, (TOK, TOK), 0)
    place = nn(jnp.where(tri, 1.0, 0.0).astype(BF16), hits.astype(BF16)) + order * PAD
    col = lax.broadcasted_iota(jnp.int32, (TOK, 32 * PAD), 1).astype(F32)
    w = jnp.zeros((TOK, 32 * PAD), F32)
    for k in range(TOP):
        at = jnp.sum(jnp.where(names[:, k : k + 1] == lane, place, 0.0), axis=1, keepdims=True)
        w = w + jnp.where(col == at, gw[:, k : k + 1], 0.0)
    for i in range(3):
        piece = w.astype(BF16)
        wmat[pl.ds(i * TOK, TOK), :] = piece
        w = w - piece.astype(F32)

    for q in (0, 1):
        y_copy(1, q).wait_recv()
        sib_copy(0, 1, q).start()
        x_copy(1, 0, q).wait_recv()
        sib_copy(0, 2, q).start()
        y_copy(0, q).wait_recv()
        sib_copy(0, 3, q).start()
        y_copy(2, q).start()
    x3_copy(0).start()
    for cp in weights:
        cp.wait()
    for q in (0, 1):
        for i in range(4):
            sib_copy(0, i, q).wait_recv()
    gather(0)
    stage_0(0)
    for q in (0, 1):
        y_copy(2, q).wait_recv()
    for dy in (2, 1, 3):
        for d in (0, 1):
            x_copy(d, dy).start()
    sib_copy(1, 1).start()
    stage(0, 1)

    def last_sum(g):
        for j in range(SRC):
            n = g * SRC + j
            pltpu.make_async_copy(rbuf.at[n], rbuf.at[n], rt_rs.at[n]).wait()
        rows = rbuf[pl.ds(g * SRC, SRC)].reshape(SRC * PAD, DC)
        parts = nn(wmat[:, pl.ds(g * SRC * PAD, SRC * PAD)], rows)
        parts = parts[2 * TOK :] + parts[TOK : 2 * TOK] + parts[:TOK]
        out_ref[...] = parts if g == 0 else out_ref[...] + parts

    def turn(i, _):
        factors = (i >= 1) & (i <= NG)

        @pl.when(i < NG)
        def _():
            stage(i, 2)

        @pl.when(i == NG + 1)
        def _():
            for g in range(NG - 1):
                last_sum(g)

        @pl.when(i >= 2)
        def _():
            last_stage(i - 2)

        @pl.when(i == 0)
        def _():
            for q in (0, 1):
                x_copy(0, 0, q).wait_recv()
            sib_copy(1, 0).start()
            x3_copy(0).wait_recv()
            sib_copy(1, 2).start()
            x_copy(0, 2).wait_recv()
            sib_copy(1, 3).start()
            x3_copy(2).start()
            for j in range(4):
                sib_copy(1, j).wait_recv()

        @pl.when(i == 1)
        def _():
            for dy in (1, 3, 2):
                x3_copy(dy).wait_recv()
                sib_copy(2, slot(2, dy)[1]).start()
            for j in range(4):
                sib_copy(2, j).wait_recv()

        @pl.when(i == 2)
        def _():
            for j in range(4):
                sib_copy(3, j).wait_recv()

        @pl.when(i < NG - 1)
        def _():
            gather(i + 1)
            stage_0(i + 1)

        @pl.when(factors)
        def _():
            gather_stage(i - 1, 1)

        @pl.when(i < NG)
        def _():
            stage(i, 3)

        @pl.when(factors)
        def _():
            gather_stage(i - 1, 2)

        @pl.when(i < NG - 1)
        def _():
            stage(i + 1, 1)

        @pl.when(i == 0)
        def _():
            x_copy(0, 3).wait_recv()
            x3_copy(3).start()
            x_copy(1, 1).wait_recv()
            x3_copy(1).start()
            x_copy(1, 2).wait_recv()
            sib_copy(2, 0).start()
            x_copy(1, 3).wait_recv()
            x_copy(0, 1).wait_recv()
            for j in range(4):
                sib_copy(3, j).start()

        @pl.when(i < NG)
        def _():
            stage_4(i)

        @pl.when(factors)
        def _():
            gather_stage(i - 1, 3)

        return 0

    lax.fori_loop(0, NG + 2, turn, 0)

    for q in (0, 1):
        for i in range(3):
            y_copy(i, q).wait_send()
        for d in (0, 1):
            x_copy(d, 0, q).wait_send()
        for i in range(4):
            sib_copy(0, i, q).wait_send()
    for i in range(4):
        x3_copy(i).wait_send()
        for g in range(1, NG):
            sib_copy(g, i).wait_send()
        for d in (0, 1):
            if i:
                x_copy(d, i).wait_send()

    def left(g, _):
        for d in (0, 1):
            for k in range(4):
                for h in (0, 1):
                    if k > 0 or h == d:

                        @pl.when(g >= 2)
                        def _():
                            rs_copy(g, d, k, h).wait_send()

                    if k < 3 or h == d:
                        for q in (0, 1):
                            ag_copy(g, d, k, h, q).wait_send()
        return 0

    lax.fori_loop(0, NG, left, 0)
    last_sum(NG - 1)

    for n in range(1, NG * SRC):
        back_copy(n // SRC, n % SRC).wait_send()


def shards(tokens, tangent, cotangent, routing, gate_weights, gate_proj, up_proj, down_proj):
    dma = pltpu.SemaphoreType.DMA
    anywhere = pl.BlockSpec(memory_space=pl.ANY)
    vmem = pl.BlockSpec(memory_space=pltpu.VMEM)
    return pl.pallas_call(
        kernel,
        out_shape=jax.ShapeDtypeStruct((TOK, DC), F32),
        in_specs=[anywhere] * 3 + [vmem] * 2 + [anywhere] * 3,
        out_specs=vmem,
        scratch_shapes=[
            pltpu.VMEM((DC, H), BF16),
            pltpu.VMEM((DC, H), BF16),
            pltpu.VMEM((H, DC), BF16),
            pltpu.VMEM((NG, 2, 4, BR, DC), BF16),
            pltpu.VMEM((2, 3 * GR, DC), BF16),
            pltpu.VMEM((5, SUMS * GR, CH), F32),
            pltpu.VMEM((32, MR, 128), jnp.int16),
            pltpu.VMEM((64, MR, 128), jnp.int16),
            pltpu.VMEM((NG * 16, 2 * GR, 128), BF16),
            pltpu.VMEM((GR, DC), F32),
            pltpu.VMEM((NG * SRC, PAD, DC), BF16),
            pltpu.VMEM((32, PAD, DC), BF16),
            pltpu.VMEM((3 * TOK, 32 * PAD), BF16),
            dma((3,)), dma((3,)), dma((6,)), dma((6,)), dma((10,)), dma((10,)), dma((4,)), dma((4,)),
            dma((20,)), dma((20,)), dma((32,)), dma((64,)), dma((128,)), dma((128,)), dma((32,)), dma((32,)),
        ],
        compiler_params=pltpu.CompilerParams(
            collective_id=0, has_side_effects=True, vmem_limit_bytes=61 * 1024 * 1024
        ),
        cost_estimate=pl.CostEstimate(
            flops=2 * 7 * 576 * DC * H, bytes_accessed=12_000_000, transcendentals=576 * H // NZ
        ),
    )(tokens, tangent, cotangent, routing.T, gate_weights.T, gate_proj[0], up_proj[0], down_proj[0])


def solution(mesh):
    in_specs = (
        P("expert", "dp"),
        P("expert", "dp"),
        P("expert", "dp"),
        P("expert", None),
        P("expert", None),
        P("expert", "dp", None),
        P("expert", "dp", None),
        P("expert", None, "dp"),
    )
    return jax.shard_map(
        shards, mesh=mesh, in_specs=in_specs, out_specs=P("expert", "dp"), check_vma=False
    )
```

```python
import jax
import jax.numpy as jnp
from jax import lax
from jax.experimental import pallas as pl
from jax.experimental.pallas import tpu as pltpu
from jax.sharding import PartitionSpec as P

MESH = pl.DeviceIdType.MESH
BF16 = jnp.bfloat16
F32 = jnp.float32

TOP = 8
TOK = 64
CAP = 18
DC = 896
H = 2048
NZ = 8
CH = H // NZ
NG = 4
SRC = 8
GR = SRC * CAP
SUMS = 5
EARLY = 2
CHIPS = (
    ((0, 0), (0, 1), (1, 0), (0, 3)),
    ((3, 0), (0, 2), (2, 0), (3, 2)),
    ((1, 2), (2, 1), (2, 3), (2, 2)),
    ((1, 1), (1, 3), (3, 1), (3, 3)),
)
MR = SUMS * GR + 16
BR = 16 + 3 * TOK
PARTS = (pl.ds(0, 16 + TOK), pl.ds(16 + TOK, 2 * TOK))
NEAR = 64
PAD = 32


def nt(a, b):
    return lax.dot_general(a, b, (((1,), (1,)), ((), ())), preferred_element_type=F32)


def nn(a, b):
    return jnp.dot(a, b, preferred_element_type=F32)


def kernel(
    x_ref, v_ref, c_ref, routing_ref, gw_ref, gate_ref, up_ref, down_ref, out_ref,
    gate_v, up_v, down_v, tok, xrows, part, rs_s, rs_r, fac, acc, sbuf, rbuf, wmat,
    near_s, near_r, w_sem, l_sem, near_ss, near_rs, y_ss, y_rs, x_ss, x_rs, x3_ss, x3_rs, sib_ss, sib_rs,
    rs_ss, rs_rs, ag_ss, ag_rs, rt_ss, rt_rs,
):
    me = lax.axis_index("dp")
    ex = lax.axis_index("expert")
    px = ex // 8
    py = (ex // 2) % 4
    pc = ex % 2

    def at_xy(dx, dy, dc):
        return (me, (((px + dx + 4) % 4) * 4 + (py + dy + 4) % 4) * 2 + (pc + dc) % 2)

    z_dev = ((me + NZ - 1) % NZ, ex), ((me + 1) % NZ, ex)
    y_dev = at_xy(0, 1, 0), at_xy(0, 3, 0)
    x_dev = at_xy(1, 0, 0), at_xy(3, 0, 0)
    sib_dev = at_xy(0, 0, 1)

    def remote(src, dst, ss, rs, dev):
        return pltpu.make_async_remote_copy(
            src_ref=src, dst_ref=dst, send_sem=ss, recv_sem=rs, device_id=dev, device_id_type=MESH
        )

    loads = [
        pltpu.make_async_copy(x_ref, tok.at[0, 0, 0, pl.ds(16, TOK)], l_sem.at[0]),
        pltpu.make_async_copy(v_ref, tok.at[0, 0, 0, pl.ds(16 + TOK, TOK)], l_sem.at[1]),
        pltpu.make_async_copy(c_ref, tok.at[0, 0, 0, pl.ds(16 + 2 * TOK, TOK)], l_sem.at[2]),
    ]
    weights = [
        pltpu.make_async_copy(gate_ref, gate_v, w_sem.at[0]),
        pltpu.make_async_copy(up_ref, up_v, w_sem.at[1]),
        pltpu.make_async_copy(down_ref, down_v, w_sem.at[2]),
    ]
    for cp in loads:
        cp.start()
    for cp in weights:
        cp.start()

    bar = pltpu.get_barrier_semaphore()
    for d in (0, 1):
        pl.semaphore_signal(bar, 1, device_id=z_dev[d], device_id_type=MESH)

    def greet(o, _):
        pl.semaphore_signal(bar, 1, device_id=(me, (ex + o) % 32), device_id_type=MESH)
        return 0

    lax.fori_loop(1, 32, greet, 0)

    named = jnp.concatenate([routing_ref[...].astype(F32), jnp.full((8, TOK), -1.0, F32)], axis=0).astype(BF16)
    twice = lax.broadcasted_iota(jnp.int32, (TOK, 128), 1) % TOK == lax.broadcasted_iota(jnp.int32, (TOK, 128), 0)
    tok[0, 0, 0, pl.ds(0, 16), :] = jnp.zeros((16, DC), BF16)
    tok[0, 0, 0, pl.ds(0, 16), pl.ds(0, 128)] = nn(named, jnp.where(twice, 1.0, 0.0).astype(BF16)).astype(BF16)

    def slot(col, dy):
        return next((g, i) for g in range(NG) for i in range(4) if CHIPS[g][i] == (col, dy))

    def block(col, dy, q=None):
        g, i = slot(col, dy)
        if q is None:
            return tok.at[g, 0, i]
        return tok.at[g, 0, i, PARTS[q]]

    def y_copy(i):
        if i < 2:
            return remote(block(0, 0), block(0, 1 if i else 3), y_ss.at[i], y_rs.at[i], y_dev[i])
        q = i - 2
        return remote(block(0, 1 if q else 3, q), block(0, 2, q), y_ss.at[i], y_rs.at[i], y_dev[q])

    def x_copy(d, dy):
        i = d * 4 + dy
        return remote(block(0, dy), block(1 if d else 3, dy), x_ss.at[i], x_rs.at[i], x_dev[d])

    def x3_copy(dy):
        col, d = (1, 1) if dy < 2 else (3, 0)
        return remote(block(col, dy), block(2, dy), x3_ss.at[dy], x3_rs.at[dy], x_dev[d])

    def sib_copy(g, i):
        n = g * 4 + i
        return remote(tok.at[g, 0, i], tok.at[g, 1, i], sib_ss.at[n], sib_rs.at[n], sib_dev)

    def near_dev(j):
        dx, dy = CHIPS[0][j % 4]
        return at_xy(-dx, -dy, j // 4)

    def near_copy(j):
        return remote(near_s.at[j], near_r.at[j], near_ss.at[j], near_rs.at[j], near_dev(j))

    def rs_copy(g, d, k, h):
        s = (((g % 2) * 2 + d) * 4 + k) * 2 + h
        r = ((g * 2 + d) * 4 + k) * 2 + h
        return remote(rs_s.at[s], rs_r.at[r], rs_ss.at[s], rs_rs.at[r], z_dev[d])

    def ag_copy(g, d, k, h, q):
        i = (((g * 2 + d) * 4 + k) * 2 + h) * 2 + q
        src, dst = (k, k + 1) if d == 0 else ((8 - k) % 8, 7 - k)
        rows = pl.ds(q * GR, GR)
        return remote(
            fac.at[(g * 8 + src) * 2 + h, rows], fac.at[(g * 8 + dst) * 2 + h, rows], ag_ss.at[i], ag_rs.at[i], z_dev[d]
        )

    def back_copy(g, j):
        dx, dy = CHIPS[g][j % 4]
        n = g * SRC + j
        return remote(sbuf.at[n], rbuf.at[n], rt_ss.at[n], rt_rs.at[n], at_xy(dx, dy, j // 4))

    def gather(g):
        lane = lax.broadcasted_iota(jnp.int32, (8, 128), 1)
        tri_r = lax.broadcasted_iota(jnp.int32, (128, 128), 0)
        tri_c = lax.broadcasted_iota(jnp.int32, (128, 128), 1)
        tri = ((tri_r < tri_c) & (tri_r // 64 == tri_c // 64)).astype(F32).astype(BF16)
        row = lax.broadcasted_iota(jnp.int32, (GR, 128), 0).astype(F32)
        low = lax.broadcasted_iota(jnp.int32, (16, 128), 1) < 64
        exf = ex.astype(F32)
        hots = []
        for c in range(2):
            for p in range(2):
                ra = tok[g, c, 2 * p, pl.ds(0, 16), pl.ds(0, 128)].astype(F32)
                rb = tok[g, c, 2 * p + 1, pl.ds(0, 16), pl.ds(0, 128)].astype(F32)
                hit = jnp.where(jnp.where(low, ra, rb) == exf, 1.0, 0.0)
                hit = jnp.broadcast_to(jnp.sum(hit, axis=0, keepdims=True), (8, 128))
                rank = nn(hit.astype(BF16), tri)
                first = (CAP * (4 * c + 2 * p) + CAP * (lane // 64)).astype(F32)
                target = jnp.where(hit > 0.5, rank + first, -1.0)
                hots.append(jnp.where(row == target[0:1], 1.0, 0.0).astype(BF16))
        hot = jnp.concatenate(hots, axis=1)
        for a in range(3):
            rows = jnp.concatenate(
                [tok[g, c, y, pl.ds(16 + a * TOK, TOK), :] for c in range(2) for y in range(4)], axis=0
            )
            xrows[g % 2, pl.ds(a * GR, GR), :] = nn(hot, rows).astype(BF16)

    def gather_near():
        r = lax.broadcasted_iota(jnp.int32, (3 * GR, SRC * NEAR), 0)
        q = lax.broadcasted_iota(jnp.int32, (3 * GR, SRC * NEAR), 1)
        from_ = (r % GR) // CAP * NEAR + r // GR * CAP + r % CAP
        hot = jnp.where(q == from_, 1.0, 0.0).astype(BF16)
        xrows[0] = nn(hot, jnp.concatenate([near_r[j] for j in range(SRC)], axis=0)).astype(BF16)

    def products(g, d, chunk):
        first = pl.multiple_of(chunk * CH, CH)
        cols = pl.ds(first, CH)
        xv = xrows[g % 2, pl.ds(0, 2 * GR), :]
        part[d, pl.ds(0, 2 * GR), :] = nn(xv, gate_v[:, cols])
        part[d, pl.ds(2 * GR, 2 * GR), :] = nn(xv, up_v[:, cols])
        part[d, pl.ds(4 * GR, GR), :] = nt(xrows[g % 2, pl.ds(2 * GR, GR), :], down_v[cols, :])

    def scales(r):
        return jnp.exp2(rs_r[r, pl.ds(SUMS * GR, 16), :].astype(F32) * (1.0 / 256.0))

    def send_sums(g, d, k, h, came):
        s = (((g % 2) * 2 + d) * 4 + k) * 2 + h
        own = 2 if k == 0 else 3 + d if k == 1 else d

        @pl.when(g >= 2)
        def _():
            rs_copy(g, d, k, h).wait_send()

        r = ((g * 2 + d) * 4 + k - 1) * 2 + h
        if came:
            rs_copy(g, d, k - 1, h).wait_recv()
            sc = scales(r)
        codes = jnp.zeros((16, 128), F32)
        at = lax.broadcasted_iota(jnp.int32, (16, 128), 0)
        for p in range(SUMS):
            rows = pl.ds(p * GR, GR)
            blk = part[own, rows, pl.ds(h * 128, 128)]
            if came:
                blk = blk + rs_r[r, rows, :].astype(F32) * sc[p : p + 1]
            most = jnp.max(jnp.abs(blk), axis=0, keepdims=True)
            code = jnp.ceil(256.0 * jnp.log2(jnp.maximum(most, 1e-30) * (1.0 / 32760.0)))
            inv = jnp.exp2(code * (-1.0 / 256.0))
            rs_s[s, rows, :] = jnp.round(blk * inv).astype(jnp.int32).astype(jnp.int16)
            codes = jnp.where(at == p, code, codes)
        rs_s[s, pl.ds(SUMS * GR, 16), :] = codes.astype(jnp.int32).astype(jnp.int16)
        rs_copy(g, d, k, h).start()

    def stage_0(g):
        products(g, 2, (me + 4) % NZ)
        for d in (0, 1):
            send_sums(g, d, 0, d, False)
        products(g, 3, (me + NZ - 3) % NZ)
        products(g, 4, (me + 3) % NZ)
        for d in (0, 1):
            send_sums(g, d, 1, 1 - d, False)

    def stage(g, k):
        if k == 1:
            for d in (0, 1):
                send_sums(g, d, 1, d, True)
            return
        products(g, 0, (me + NZ - (4 - k)) % NZ)
        products(g, 1, (me + 4 - k) % NZ)
        for h in (1, 0):
            for d in (0, 1):
                send_sums(g, d, k, h if d == 0 else 1 - h, True)

    def stage_4(g):
        products(g, 2, me)
        for h in (0, 1):
            total = []
            r = [((g * 2 + d) * 4 + 3) * 2 + h for d in (0, 1)]
            for d in (0, 1):
                rs_copy(g, d, 3, h).wait_recv()
            sc = [scales(r[0]), scales(r[1])]
            for p in range(SUMS):
                rows = pl.ds(p * GR, GR)
                blk = part[2, rows, pl.ds(h * 128, 128)]
                for d in (0, 1):
                    blk = blk + rs_r[r[d], rows, :].astype(F32) * sc[d][p : p + 1]
                total.append(blk)
            a, da, b, db, dh = total
            sig = 1.0 / (1.0 + jnp.exp(-a))
            s1 = sig * (1.0 + a * (1.0 - sig))
            s2 = sig * (1.0 - sig) * (2.0 + a * (1.0 - 2.0 * sig))
            fac[g * 16 + h, pl.ds(0, GR), :] = (dh * (s2 * da * b + s1 * db)).astype(BF16)
            fac[g * 16 + h, pl.ds(GR, GR), :] = (dh * s1 * da).astype(BF16)
            for q in (0, 1):
                for d in (0, 1):
                    ag_copy(g, d, 0, h, q).start()

    def add_rows(g, r, new):
        cols = pl.ds(pl.multiple_of(((me + r) % NZ) * CH, CH), CH)
        f = jnp.concatenate([fac[(g * 8 + r) * 2], fac[(g * 8 + r) * 2 + 1]], axis=1)
        more = nt(f[0:GR], gate_v[:, cols]) + nt(f[GR:], up_v[:, cols])
        acc[...] = more if new else acc[...] + more

    def gather_stage(g, k):
        for h in (0, 1):
            for q in (0, 1):
                for d in (0, 1):
                    ag_copy(g, d, k - 1, h, q).wait_recv()
                    if k < 3 or h == d:
                        ag_copy(g, d, k, h, q).start()
        if k == 1:
            add_rows(g, 0, True)
        add_rows(g, k, False)
        add_rows(g, 8 - k, False)

    def last_stage(g):
        for q in (0, 1):
            for d in (0, 1):
                ag_copy(g, d, 3, d, q).wait_recv()
        add_rows(g, 4, False)
        rows = acc[...].astype(BF16)
        o = lax.broadcasted_iota(jnp.int32, (SRC * PAD, GR), 0)
        i = lax.broadcasted_iota(jnp.int32, (SRC * PAD, GR), 1)
        hot = jnp.where((o % PAD < CAP) & (i == (o // PAD) * CAP + o % PAD), 1.0, 0.0).astype(BF16)
        spread = nn(hot, rows).astype(BF16)
        for j in range(SRC):
            sbuf[g * SRC + j] = spread[j * PAD : (j + 1) * PAD]
        for at in range(NG):

            @pl.when(g == at)
            def _():
                for j in range(SRC):
                    if at == 0 and j == 0:
                        pltpu.make_async_copy(sbuf.at[0], rbuf.at[0], rt_rs.at[0]).start()
                    else:
                        back_copy(at, j).start()

    thrice = lax.broadcasted_iota(jnp.int32, (TOK, 3 * TOK), 1) % TOK == lax.broadcasted_iota(jnp.int32, (TOK, 3 * TOK), 0)
    wide = nn(named, jnp.where(thrice, 1.0, 0.0).astype(BF16))
    at = lax.broadcasted_iota(jnp.int32, (SRC, 3 * TOK), 0)
    hits = jnp.zeros((SRC, 3 * TOK), F32)
    for j in range(SRC):
        hit = jnp.sum(jnp.where(wide == near_dev(j)[1].astype(F32), 1.0, 0.0), axis=0, keepdims=True)
        hits = jnp.where(at == j, hit, hits)
    tri_r = lax.broadcasted_iota(jnp.int32, (3 * TOK, 3 * TOK), 0)
    tri_c = lax.broadcasted_iota(jnp.int32, (3 * TOK, 3 * TOK), 1)
    tri = jnp.where((tri_r < tri_c) & (tri_r // TOK == tri_c // TOK), 1.0, 0.0).astype(BF16)
    first = (lax.broadcasted_iota(jnp.int32, (SRC, 3 * TOK), 1) // TOK * CAP).astype(F32)
    target = jnp.where(hits > 0.5, nn(hits.astype(BF16), tri) + first, -1.0)
    row = lax.broadcasted_iota(jnp.int32, (NEAR, 3 * TOK), 0).astype(F32)
    hot = jnp.concatenate(
        [jnp.where(row == target[j : j + 1], 1.0, 0.0).astype(BF16) for j in range(SRC)], axis=0
    )
    for cp in loads:
        cp.wait()
    near = nn(hot, tok[0, 0, 0, pl.ds(16, 3 * TOK), :]).astype(BF16)
    for j in range(SRC):
        near_s[j] = near[j * NEAR : (j + 1) * NEAR]
    near_r[0] = near[0:NEAR]
    pl.semaphore_wait(bar, 33)

    for j in (1, 2, 3, 5, 6, 7, 4):
        near_copy(j).start()
    for i in (0, 1):
        y_copy(i).start()
    for d in (1, 0):
        x_copy(d, 0).start()

    same = lax.broadcasted_iota(jnp.int32, (TOK, TOK), 0) == lax.broadcasted_iota(jnp.int32, (TOK, TOK), 1)
    same = jnp.where(same, 1.0, 0.0).astype(BF16)
    names = nt(same, routing_ref[...].astype(F32).astype(BF16))
    rest = gw_ref[...]
    gw = jnp.zeros((TOK, TOP), F32)
    for i in range(3):
        piece = rest.astype(BF16)
        gw = gw + nt(same, piece)
        rest = rest - piece.astype(F32)
    hits = jnp.zeros((TOK, 128), F32)
    lane = lax.broadcasted_iota(jnp.int32, (TOK, 128), 1).astype(F32)
    for k in range(TOP):
        hits = hits + jnp.where(names[:, k : k + 1] == lane, 1.0, 0.0)
    order = jnp.zeros((TOK, 128), F32)
    for n in range(NG * SRC):
        dx, dy = CHIPS[n // SRC][n % 4]
        order = jnp.where(lane == at_xy(-dx, -dy, n % SRC // 4)[1].astype(F32), float(n), order)
    tri = lax.broadcasted_iota(jnp.int32, (TOK, TOK), 1) < lax.broadcasted_iota(jnp.int32, (TOK, TOK), 0)
    place = nn(jnp.where(tri, 1.0, 0.0).astype(BF16), hits.astype(BF16)) + order * PAD
    col = lax.broadcasted_iota(jnp.int32, (TOK, 32 * PAD), 1).astype(F32)
    w = jnp.zeros((TOK, 32 * PAD), F32)
    for k in range(TOP):
        at = jnp.sum(jnp.where(names[:, k : k + 1] == lane, place, 0.0), axis=1, keepdims=True)
        w = w + jnp.where(col == at, gw[:, k : k + 1], 0.0)
    for i in range(3):
        piece = w.astype(BF16)
        wmat[pl.ds(i * TOK, TOK), :] = piece
        w = w - piece.astype(F32)

    for cp in weights:
        cp.wait()
    for j in (4, 1, 2, 3, 5, 6, 7):
        near_copy(j).wait_recv()
    gather_near()
    stage_0(0)
    stage(0, 1)
    for i in (0, 1):
        y_copy(i).wait_recv()
        y_copy(2 + i).start()
    for dy in (1, 3):
        x_copy(0, dy).start()
    x_copy(1, 0).wait_recv()
    x3_copy(0).start()
    for dy in (1, 3):
        x_copy(1, dy).start()

    def last_sum(g):
        for j in range(SRC):
            n = g * SRC + j
            pltpu.make_async_copy(rbuf.at[n], rbuf.at[n], rt_rs.at[n]).wait()
        rows = rbuf[pl.ds(g * SRC, SRC)].reshape(SRC * PAD, DC)
        parts = nn(wmat[:, pl.ds(g * SRC * PAD, SRC * PAD)], rows)
        parts = parts[2 * TOK :] + parts[TOK : 2 * TOK] + parts[:TOK]
        out_ref[...] = parts if g == 0 else out_ref[...] + parts

    def turn(i, _):
        factors = (i >= 1) & (i <= NG)

        @pl.when(i < NG)
        def _():
            stage(i, 2)

        @pl.when(i == NG + 1)
        def _():
            for g in range(NG - 1):
                last_sum(g)

        @pl.when(i >= 2)
        def _():
            last_stage(i - 2)

        @pl.when(i == 0)
        def _():
            y_copy(2).wait_recv()
            y_copy(3).wait_recv()
            for d in (0, 1):
                x_copy(d, 2).start()
            sib_copy(1, slot(0, 2)[1]).start()
            stage(0, 3)
            x_copy(0, 0).wait_recv()
            sib_copy(1, slot(3, 0)[1]).start()
            x3_copy(0).wait_recv()
            sib_copy(1, slot(2, 0)[1]).start()
            x_copy(0, EARLY).wait_recv()
            sib_copy(1, slot(3, EARLY)[1]).start()
            for j in range(4):
                sib_copy(1, j).wait_recv()

        @pl.when(i == 1)
        def _():
            for dy in (1, 3, 2):
                x3_copy(dy).wait_recv()
                sib_copy(2, slot(2, dy)[1]).start()
            for j in range(4):
                sib_copy(2, j).wait_recv()

        @pl.when(i == 2)
        def _():
            for j in range(4):
                sib_copy(3, j).wait_recv()

        @pl.when(i < NG - 1)
        def _():
            gather(i + 1)
            stage_0(i + 1)

        @pl.when(factors)
        def _():
            gather_stage(i - 1, 1)

        @pl.when((i > 0) & (i < NG))
        def _():
            stage(i, 3)

        @pl.when(factors)
        def _():
            gather_stage(i - 1, 2)

        @pl.when(i < NG - 1)
        def _():
            stage(i + 1, 1)

        @pl.when(i == 0)
        def _():
            for dy in (1, 3, 2):
                if dy != EARLY:
                    x_copy(0, dy).wait_recv()
            x3_copy(3).start()
            x3_copy(2).start()
            for dy in (1, 3, 2):
                x_copy(1, dy).wait_recv()
                if dy == 1:
                    x3_copy(1).start()
            sib_copy(2, slot(1, 2)[1]).start()
            for j in range(4):
                sib_copy(3, j).start()

        @pl.when(i < NG)
        def _():
            stage_4(i)

        @pl.when(factors)
        def _():
            gather_stage(i - 1, 3)

        return 0

    lax.fori_loop(0, NG + 2, turn, 0)

    for j in range(1, SRC):
        near_copy(j).wait_send()
    for i in range(4):
        y_copy(i).wait_send()
        x3_copy(i).wait_send()
        for g in range(1, NG):
            sib_copy(g, i).wait_send()
        for d in (0, 1):
            x_copy(d, i).wait_send()

    def left(g, _):
        for d in (0, 1):
            for k in range(4):
                for h in (0, 1):
                    if k > 0 or h == d:

                        @pl.when(g >= 2)
                        def _():
                            rs_copy(g, d, k, h).wait_send()

                    if k < 3 or h == d:
                        for q in (0, 1):
                            ag_copy(g, d, k, h, q).wait_send()
        return 0

    lax.fori_loop(0, NG, left, 0)
    last_sum(NG - 1)

    for n in range(1, NG * SRC):
        back_copy(n // SRC, n % SRC).wait_send()


def shards(tokens, tangent, cotangent, routing, gate_weights, gate_proj, up_proj, down_proj):
    dma = pltpu.SemaphoreType.DMA
    anywhere = pl.BlockSpec(memory_space=pl.ANY)
    vmem = pl.BlockSpec(memory_space=pltpu.VMEM)
    return pl.pallas_call(
        kernel,
        out_shape=jax.ShapeDtypeStruct((TOK, DC), F32),
        in_specs=[anywhere] * 3 + [vmem] * 2 + [anywhere] * 3,
        out_specs=vmem,
        scratch_shapes=[
            pltpu.VMEM((DC, H), BF16),
            pltpu.VMEM((DC, H), BF16),
            pltpu.VMEM((H, DC), BF16),
            pltpu.VMEM((NG, 2, 4, BR, DC), BF16),
            pltpu.VMEM((2, 3 * GR, DC), BF16),
            pltpu.VMEM((5, SUMS * GR, CH), F32),
            pltpu.VMEM((32, MR, 128), jnp.int16),
            pltpu.VMEM((64, MR, 128), jnp.int16),
            pltpu.VMEM((NG * 16, 2 * GR, 128), BF16),
            pltpu.VMEM((GR, DC), F32),
            pltpu.VMEM((NG * SRC, PAD, DC), BF16),
            pltpu.VMEM((32, PAD, DC), BF16),
            pltpu.VMEM((3 * TOK, 32 * PAD), BF16),
            pltpu.VMEM((SRC, NEAR, DC), BF16),
            pltpu.VMEM((SRC, NEAR, DC), BF16),
            dma((3,)), dma((3,)), dma((8,)), dma((8,)), dma((4,)), dma((4,)), dma((8,)), dma((8,)), dma((4,)), dma((4,)),
            dma((16,)), dma((16,)), dma((32,)), dma((64,)), dma((128,)), dma((128,)), dma((32,)), dma((32,)),
        ],
        compiler_params=pltpu.CompilerParams(
            collective_id=0, has_side_effects=True, vmem_limit_bytes=61 * 1024 * 1024
        ),
        cost_estimate=pl.CostEstimate(
            flops=2 * 7 * 576 * DC * H, bytes_accessed=12_000_000, transcendentals=576 * H // NZ
        ),
    )(tokens, tangent, cotangent, routing.T, gate_weights.T, gate_proj[0], up_proj[0], down_proj[0])


def solution(mesh):
    in_specs = (
        P("expert", "dp"),
        P("expert", "dp"),
        P("expert", "dp"),
        P("expert", None),
        P("expert", None),
        P("expert", "dp", None),
        P("expert", "dp", None),
        P("expert", None, "dp"),
    )
    return jax.shard_map(
        shards, mesh=mesh, in_specs=in_specs, out_specs=P("expert", "dp"), check_vma=False
    )
```

```python
import jax
import jax.numpy as jnp
from jax import lax
from jax.experimental import pallas as pl
from jax.experimental.pallas import tpu as pltpu
from jax.sharding import PartitionSpec as P

MESH = pl.DeviceIdType.MESH
BF16 = jnp.bfloat16
F32 = jnp.float32

TOP = 8
TOK = 64
CAP = 18
DC = 896
H = 2048
NZ = 8
CH = H // NZ
NG = 4
SRC = 8
GR = SRC * CAP
SUMS = 5
EARLY = 2
CHIPS = (
    ((0, 0), (0, 1), (1, 0), (0, 3)),
    ((3, 0), (0, 2), (2, 0), (3, 2)),
    ((1, 2), (2, 1), (2, 3), (2, 2)),
    ((1, 1), (1, 3), (3, 1), (3, 3)),
)
MR = SUMS * GR + 16
BR = 16 + 3 * TOK
PARTS = (pl.ds(0, 16 + TOK), pl.ds(16 + TOK, 2 * TOK))
NEAR = 64
PAD = 32


def nt(a, b):
    return lax.dot_general(a, b, (((1,), (1,)), ((), ())), preferred_element_type=F32)


def nn(a, b):
    return jnp.dot(a, b, preferred_element_type=F32)


def kernel(
    x_ref, v_ref, c_ref, routing_ref, gw_ref, gate_ref, up_ref, down_ref, out_ref,
    gate_v, up_v, down_v, tok, xrows, part, rs_s, rs_r, fac, acc, sbuf, rbuf, wmat,
    near_s, near_r, w_sem, l_sem, near_ss, near_rs, y_ss, y_rs, x_ss, x_rs, x3_ss, x3_rs, sib_ss, sib_rs,
    rs_ss, rs_rs, ag_ss, ag_rs, rt_ss, rt_rs,
):
    me = lax.axis_index("dp")
    ex = lax.axis_index("expert")
    px = ex // 8
    py = (ex // 2) % 4
    pc = ex % 2

    def at_xy(dx, dy, dc):
        return (me, (((px + dx + 4) % 4) * 4 + (py + dy + 4) % 4) * 2 + (pc + dc) % 2)

    z_dev = ((me + NZ - 1) % NZ, ex), ((me + 1) % NZ, ex)
    y_dev = at_xy(0, 1, 0), at_xy(0, 3, 0)
    x_dev = at_xy(1, 0, 0), at_xy(3, 0, 0)
    sib_dev = at_xy(0, 0, 1)

    def remote(src, dst, ss, rs, dev):
        return pltpu.make_async_remote_copy(
            src_ref=src, dst_ref=dst, send_sem=ss, recv_sem=rs, device_id=dev, device_id_type=MESH
        )

    loads = [
        pltpu.make_async_copy(x_ref, tok.at[0, 0, 0, pl.ds(16, TOK)], l_sem.at[0]),
        pltpu.make_async_copy(v_ref, tok.at[0, 0, 0, pl.ds(16 + TOK, TOK)], l_sem.at[1]),
        pltpu.make_async_copy(c_ref, tok.at[0, 0, 0, pl.ds(16 + 2 * TOK, TOK)], l_sem.at[2]),
    ]
    weights = [
        pltpu.make_async_copy(gate_ref, gate_v, w_sem.at[0]),
        pltpu.make_async_copy(up_ref, up_v, w_sem.at[1]),
        pltpu.make_async_copy(down_ref, down_v, w_sem.at[2]),
    ]
    for cp in loads:
        cp.start()
    for cp in weights:
        cp.start()

    bar = pltpu.get_barrier_semaphore()
    for d in (0, 1):
        pl.semaphore_signal(bar, 1, device_id=z_dev[d], device_id_type=MESH)

    def greet(o, _):
        pl.semaphore_signal(bar, 1, device_id=(me, (ex + o) % 32), device_id_type=MESH)
        return 0

    lax.fori_loop(1, 32, greet, 0)

    named = jnp.concatenate([routing_ref[...].astype(F32), jnp.full((8, TOK), -1.0, F32)], axis=0).astype(BF16)
    twice = lax.broadcasted_iota(jnp.int32, (TOK, 128), 1) % TOK == lax.broadcasted_iota(jnp.int32, (TOK, 128), 0)
    tok[0, 0, 0, pl.ds(0, 16), :] = jnp.zeros((16, DC), BF16)
    tok[0, 0, 0, pl.ds(0, 16), pl.ds(0, 128)] = nn(named, jnp.where(twice, 1.0, 0.0).astype(BF16)).astype(BF16)

    def slot(col, dy):
        return next((g, i) for g in range(NG) for i in range(4) if CHIPS[g][i] == (col, dy))

    def block(col, dy, q=None):
        g, i = slot(col, dy)
        if q is None:
            return tok.at[g, 0, i]
        return tok.at[g, 0, i, PARTS[q]]

    def y_copy(i):
        if i < 2:
            return remote(block(0, 0), block(0, 1 if i else 3), y_ss.at[i], y_rs.at[i], y_dev[i])
        q = i - 2
        return remote(block(0, 1 if q else 3, q), block(0, 2, q), y_ss.at[i], y_rs.at[i], y_dev[q])

    def x_copy(d, dy):
        i = d * 4 + dy
        return remote(block(0, dy), block(1 if d else 3, dy), x_ss.at[i], x_rs.at[i], x_dev[d])

    def x3_copy(dy):
        col, d = (1, 1) if dy < 2 else (3, 0)
        return remote(block(col, dy), block(2, dy), x3_ss.at[dy], x3_rs.at[dy], x_dev[d])

    def sib_copy(g, i):
        n = g * 4 + i
        return remote(tok.at[g, 0, i], tok.at[g, 1, i], sib_ss.at[n], sib_rs.at[n], sib_dev)

    def near_dev(j):
        dx, dy = CHIPS[0][j % 4]
        return at_xy(-dx, -dy, j // 4)

    def near_copy(j):
        return remote(near_s.at[j], near_r.at[j], near_ss.at[j], near_rs.at[j], near_dev(j))

    def rs_copy(g, d, k, h):
        s = (((g % 2) * 2 + d) * 4 + k) * 2 + h
        r = ((g * 2 + d) * 4 + k) * 2 + h
        return remote(rs_s.at[s], rs_r.at[r], rs_ss.at[s], rs_rs.at[r], z_dev[d])

    def ag_copy(g, d, k, h, q):
        i = (((g * 2 + d) * 4 + k) * 2 + h) * 2 + q
        src, dst = (k, k + 1) if d == 0 else ((8 - k) % 8, 7 - k)
        rows = pl.ds(q * GR, GR)
        return remote(
            fac.at[(g * 8 + src) * 2 + h, rows], fac.at[(g * 8 + dst) * 2 + h, rows], ag_ss.at[i], ag_rs.at[i], z_dev[d]
        )

    def back_copy(g, j):
        dx, dy = CHIPS[g][j % 4]
        n = g * SRC + j
        return remote(sbuf.at[n], rbuf.at[n], rt_ss.at[n], rt_rs.at[n], at_xy(dx, dy, j // 4))

    def gather(g):
        lane = lax.broadcasted_iota(jnp.int32, (8, 128), 1)
        tri_r = lax.broadcasted_iota(jnp.int32, (128, 128), 0)
        tri_c = lax.broadcasted_iota(jnp.int32, (128, 128), 1)
        tri = ((tri_r < tri_c) & (tri_r // 64 == tri_c // 64)).astype(F32).astype(BF16)
        row = lax.broadcasted_iota(jnp.int32, (GR, 128), 0).astype(F32)
        low = lax.broadcasted_iota(jnp.int32, (16, 128), 1) < 64
        exf = ex.astype(F32)
        hots = []
        for c in range(2):
            for p in range(2):
                ra = tok[g, c, 2 * p, pl.ds(0, 16), pl.ds(0, 128)].astype(F32)
                rb = tok[g, c, 2 * p + 1, pl.ds(0, 16), pl.ds(0, 128)].astype(F32)
                hit = jnp.where(jnp.where(low, ra, rb) == exf, 1.0, 0.0)
                hit = jnp.broadcast_to(jnp.sum(hit, axis=0, keepdims=True), (8, 128))
                rank = nn(hit.astype(BF16), tri)
                first = (CAP * (4 * c + 2 * p) + CAP * (lane // 64)).astype(F32)
                target = jnp.where(hit > 0.5, rank + first, -1.0)
                hots.append(jnp.where(row == target[0:1], 1.0, 0.0).astype(BF16))
        hot = jnp.concatenate(hots, axis=1)
        for a in range(3):
            rows = jnp.concatenate(
                [tok[g, c, y, pl.ds(16 + a * TOK, TOK), :] for c in range(2) for y in range(4)], axis=0
            )
            xrows[g % 2, pl.ds(a * GR, GR), :] = nn(hot, rows).astype(BF16)

    def gather_near():
        r = lax.broadcasted_iota(jnp.int32, (3 * GR, SRC * NEAR), 0)
        q = lax.broadcasted_iota(jnp.int32, (3 * GR, SRC * NEAR), 1)
        from_ = (r % GR) // CAP * NEAR + r // GR * CAP + r % CAP
        hot = jnp.where(q == from_, 1.0, 0.0).astype(BF16)
        xrows[0] = nn(hot, jnp.concatenate([near_r[j] for j in range(SRC)], axis=0)).astype(BF16)

    def products(g, d, chunk):
        first = pl.multiple_of(chunk * CH, CH)
        cols = pl.ds(first, CH)
        xv = xrows[g % 2, pl.ds(0, 2 * GR), :]
        part[d, pl.ds(0, 2 * GR), :] = nn(xv, gate_v[:, cols])
        part[d, pl.ds(2 * GR, 2 * GR), :] = nn(xv, up_v[:, cols])
        part[d, pl.ds(4 * GR, GR), :] = nt(xrows[g % 2, pl.ds(2 * GR, GR), :], down_v[cols, :])

    def scales(r):
        return jnp.exp2(rs_r[r, pl.ds(SUMS * GR, 16), :].astype(F32) * (1.0 / 256.0))

    def send_sums(g, d, k, h, came):
        s = (((g % 2) * 2 + d) * 4 + k) * 2 + h
        own = 2 if k == 0 else 3 + d if k == 1 else d

        @pl.when(g >= 2)
        def _():
            rs_copy(g, d, k, h).wait_send()

        r = ((g * 2 + d) * 4 + k - 1) * 2 + h
        if came:
            rs_copy(g, d, k - 1, h).wait_recv()
            sc = scales(r)
        codes = jnp.zeros((16, 128), F32)
        at = lax.broadcasted_iota(jnp.int32, (16, 128), 0)
        for p in range(SUMS):
            rows = pl.ds(p * GR, GR)
            blk = part[own, rows, pl.ds(h * 128, 128)]
            if came:
                blk = blk + rs_r[r, rows, :].astype(F32) * sc[p : p + 1]
            most = jnp.max(jnp.abs(blk), axis=0, keepdims=True)
            code = jnp.ceil(256.0 * jnp.log2(jnp.maximum(most, 1e-30) * (1.0 / 32760.0)))
            inv = jnp.exp2(code * (-1.0 / 256.0))
            rs_s[s, rows, :] = jnp.round(blk * inv).astype(jnp.int32).astype(jnp.int16)
            codes = jnp.where(at == p, code, codes)
        rs_s[s, pl.ds(SUMS * GR, 16), :] = codes.astype(jnp.int32).astype(jnp.int16)
        rs_copy(g, d, k, h).start()

    def stage_0(g):
        products(g, 2, (me + 4) % NZ)
        for d in (0, 1):
            send_sums(g, d, 0, d, False)
        products(g, 3, (me + NZ - 3) % NZ)
        products(g, 4, (me + 3) % NZ)
        for d in (0, 1):
            send_sums(g, d, 1, 1 - d, False)

    def stage(g, k):
        if k == 1:
            for d in (0, 1):
                send_sums(g, d, 1, d, True)
            return
        products(g, 0, (me + NZ - (4 - k)) % NZ)
        products(g, 1, (me + 4 - k) % NZ)
        for h in (1, 0):
            for d in (0, 1):
                send_sums(g, d, k, h if d == 0 else 1 - h, True)

    def stage_4(g):
        products(g, 2, me)
        for h in (0, 1):
            total = []
            r = [((g * 2 + d) * 4 + 3) * 2 + h for d in (0, 1)]
            for d in (0, 1):
                rs_copy(g, d, 3, h).wait_recv()
            sc = [scales(r[0]), scales(r[1])]
            for p in range(SUMS):
                rows = pl.ds(p * GR, GR)
                blk = part[2, rows, pl.ds(h * 128, 128)]
                for d in (0, 1):
                    blk = blk + rs_r[r[d], rows, :].astype(F32) * sc[d][p : p + 1]
                total.append(blk)
            a, da, b, db, dh = total
            sig = 1.0 / (1.0 + jnp.exp(-a))
            s1 = sig * (1.0 + a * (1.0 - sig))
            s2 = sig * (1.0 - sig) * (2.0 + a * (1.0 - 2.0 * sig))
            fac[g * 16 + h, pl.ds(0, GR), :] = (dh * (s2 * da * b + s1 * db)).astype(BF16)
            fac[g * 16 + h, pl.ds(GR, GR), :] = (dh * s1 * da).astype(BF16)
            for q in (0, 1):
                for d in (0, 1):
                    ag_copy(g, d, 0, h, q).start()

    def add_rows(g, r, new):
        cols = pl.ds(pl.multiple_of(((me + r) % NZ) * CH, CH), CH)
        f = jnp.concatenate([fac[(g * 8 + r) * 2], fac[(g * 8 + r) * 2 + 1]], axis=1)
        more = nt(f[0:GR], gate_v[:, cols]) + nt(f[GR:], up_v[:, cols])
        acc[...] = more if new else acc[...] + more

    def gather_stage(g, k):
        for h in (0, 1):
            for q in (0, 1):
                for d in (0, 1):
                    ag_copy(g, d, k - 1, h, q).wait_recv()
                    if k < 3 or h == d:
                        ag_copy(g, d, k, h, q).start()
        if k == 1:
            add_rows(g, 0, True)
        add_rows(g, k, False)
        add_rows(g, 8 - k, False)

    def last_stage(g):
        for q in (0, 1):
            for d in (0, 1):
                ag_copy(g, d, 3, d, q).wait_recv()
        add_rows(g, 4, False)
        rows = acc[...].astype(BF16)
        o = lax.broadcasted_iota(jnp.int32, (SRC * PAD, GR), 0)
        i = lax.broadcasted_iota(jnp.int32, (SRC * PAD, GR), 1)
        hot = jnp.where((o % PAD < CAP) & (i == (o // PAD) * CAP + o % PAD), 1.0, 0.0).astype(BF16)
        spread = nn(hot, rows).astype(BF16)
        for j in range(SRC):
            sbuf[g * SRC + j] = spread[j * PAD : (j + 1) * PAD]
        for at in range(NG):

            @pl.when(g == at)
            def _():
                for j in range(SRC):
                    if at == 0 and j == 0:
                        pltpu.make_async_copy(sbuf.at[0], rbuf.at[0], rt_rs.at[0]).start()
                    else:
                        back_copy(at, j).start()

    thrice = lax.broadcasted_iota(jnp.int32, (TOK, 3 * TOK), 1) % TOK == lax.broadcasted_iota(jnp.int32, (TOK, 3 * TOK), 0)
    wide = nn(named, jnp.where(thrice, 1.0, 0.0).astype(BF16))
    at = lax.broadcasted_iota(jnp.int32, (SRC, 3 * TOK), 0)
    hits = jnp.zeros((SRC, 3 * TOK), F32)
    for j in range(SRC):
        hit = jnp.sum(jnp.where(wide == near_dev(j)[1].astype(F32), 1.0, 0.0), axis=0, keepdims=True)
        hits = jnp.where(at == j, hit, hits)
    tri_r = lax.broadcasted_iota(jnp.int32, (3 * TOK, 3 * TOK), 0)
    tri_c = lax.broadcasted_iota(jnp.int32, (3 * TOK, 3 * TOK), 1)
    tri = jnp.where((tri_r < tri_c) & (tri_r // TOK == tri_c // TOK), 1.0, 0.0).astype(BF16)
    first = (lax.broadcasted_iota(jnp.int32, (SRC, 3 * TOK), 1) // TOK * CAP).astype(F32)
    target = jnp.where(hits > 0.5, nn(hits.astype(BF16), tri) + first, -1.0)
    row = lax.broadcasted_iota(jnp.int32, (NEAR, 3 * TOK), 0).astype(F32)
    hot = jnp.concatenate(
        [jnp.where(row == target[j : j + 1], 1.0, 0.0).astype(BF16) for j in range(SRC)], axis=0
    )
    for cp in loads:
        cp.wait()
    near = nn(hot, tok[0, 0, 0, pl.ds(16, 3 * TOK), :]).astype(BF16)
    for j in range(SRC):
        near_s[j] = near[j * NEAR : (j + 1) * NEAR]
    near_r[0] = near[0:NEAR]
    pl.semaphore_wait(bar, 33)

    for j in (1, 2, 3, 5, 6, 7, 4):
        near_copy(j).start()
    for i in (0, 1):
        y_copy(i).start()
    for d in (1, 0):
        x_copy(d, 0).start()

    same = lax.broadcasted_iota(jnp.int32, (TOK, TOK), 0) == lax.broadcasted_iota(jnp.int32, (TOK, TOK), 1)
    same = jnp.where(same, 1.0, 0.0).astype(BF16)
    names = nt(same, routing_ref[...].astype(F32).astype(BF16))
    rest = gw_ref[...]
    gw = jnp.zeros((TOK, TOP), F32)
    for i in range(3):
        piece = rest.astype(BF16)
        gw = gw + nt(same, piece)
        rest = rest - piece.astype(F32)
    hits = jnp.zeros((TOK, 128), F32)
    lane = lax.broadcasted_iota(jnp.int32, (TOK, 128), 1).astype(F32)
    for k in range(TOP):
        hits = hits + jnp.where(names[:, k : k + 1] == lane, 1.0, 0.0)
    order = jnp.zeros((TOK, 128), F32)
    for n in range(NG * SRC):
        dx, dy = CHIPS[n // SRC][n % 4]
        order = jnp.where(lane == at_xy(-dx, -dy, n % SRC // 4)[1].astype(F32), float(n), order)
    tri = lax.broadcasted_iota(jnp.int32, (TOK, TOK), 1) < lax.broadcasted_iota(jnp.int32, (TOK, TOK), 0)
    place = nn(jnp.where(tri, 1.0, 0.0).astype(BF16), hits.astype(BF16)) + order * PAD
    col = lax.broadcasted_iota(jnp.int32, (TOK, 32 * PAD), 1).astype(F32)
    w = jnp.zeros((TOK, 32 * PAD), F32)
    for k in range(TOP):
        at = jnp.sum(jnp.where(names[:, k : k + 1] == lane, place, 0.0), axis=1, keepdims=True)
        w = w + jnp.where(col == at, gw[:, k : k + 1], 0.0)
    for i in range(3):
        piece = w.astype(BF16)
        wmat[pl.ds(i * TOK, TOK), :] = piece
        w = w - piece.astype(F32)

    for cp in weights:
        cp.wait()
    for j in (4, 1, 2, 3, 5, 6, 7):
        near_copy(j).wait_recv()
    gather_near()
    stage_0(0)
    stage(0, 1)
    for i in (0, 1):
        y_copy(i).wait_recv()
        y_copy(2 + i).start()
    x_copy(1, 0).wait_recv()
    x3_copy(0).start()
    for dy in (1, 3):
        x_copy(1, dy).start()

    def last_sum(g):
        for j in range(SRC):
            n = g * SRC + j
            pltpu.make_async_copy(rbuf.at[n], rbuf.at[n], rt_rs.at[n]).wait()
        rows = rbuf[pl.ds(g * SRC, SRC)].reshape(SRC * PAD, DC)
        parts = nn(wmat[:, pl.ds(g * SRC * PAD, SRC * PAD)], rows)
        parts = parts[2 * TOK :] + parts[TOK : 2 * TOK] + parts[:TOK]
        out_ref[...] = parts if g == 0 else out_ref[...] + parts

    def turn(i, _):
        factors = (i >= 1) & (i <= NG)

        @pl.when(i < NG)
        def _():
            stage(i, 2)

        @pl.when(i == NG + 1)
        def _():
            for g in range(NG - 1):
                last_sum(g)

        @pl.when(i >= 2)
        def _():
            last_stage(i - 2)

        @pl.when(i == 0)
        def _():
            y_copy(2).wait_recv()
            y_copy(3).wait_recv()
            for d in (0, 1):
                x_copy(d, 2).start()
            for dy in (1, 3):
                x_copy(0, dy).start()
            sib_copy(1, slot(0, 2)[1]).start()
            stage(0, 3)
            x_copy(0, 0).wait_recv()
            sib_copy(1, slot(3, 0)[1]).start()
            x3_copy(0).wait_recv()
            sib_copy(1, slot(2, 0)[1]).start()
            x_copy(0, EARLY).wait_recv()
            sib_copy(1, slot(3, EARLY)[1]).start()
            for j in range(4):
                sib_copy(1, j).wait_recv()

        @pl.when(i == 1)
        def _():
            for dy in (1, 3, 2):
                x3_copy(dy).wait_recv()
                sib_copy(2, slot(2, dy)[1]).start()
            for j in range(4):
                sib_copy(2, j).wait_recv()

        @pl.when(i == 2)
        def _():
            for j in range(4):
                sib_copy(3, j).wait_recv()

        @pl.when(i < NG - 1)
        def _():
            gather(i + 1)
            stage_0(i + 1)

        @pl.when(factors)
        def _():
            gather_stage(i - 1, 1)

        @pl.when((i > 0) & (i < NG))
        def _():
            stage(i, 3)

        @pl.when(factors)
        def _():
            gather_stage(i - 1, 2)

        @pl.when(i < NG - 1)
        def _():
            stage(i + 1, 1)

        @pl.when(i == 0)
        def _():
            for dy in (1, 3, 2):
                if dy != EARLY:
                    x_copy(0, dy).wait_recv()
            x3_copy(3).start()
            x3_copy(2).start()
            for dy in (1, 3, 2):
                x_copy(1, dy).wait_recv()
                if dy == 1:
                    x3_copy(1).start()
            sib_copy(2, slot(1, 2)[1]).start()
            for j in range(4):
                sib_copy(3, j).start()

        @pl.when(i < NG)
        def _():
            stage_4(i)

        @pl.when(factors)
        def _():
            gather_stage(i - 1, 3)

        return 0

    lax.fori_loop(0, NG + 2, turn, 0)

    for j in range(1, SRC):
        near_copy(j).wait_send()
    for i in range(4):
        y_copy(i).wait_send()
        x3_copy(i).wait_send()
        for g in range(1, NG):
            sib_copy(g, i).wait_send()
        for d in (0, 1):
            x_copy(d, i).wait_send()

    def left(g, _):
        for d in (0, 1):
            for k in range(4):
                for h in (0, 1):
                    if k > 0 or h == d:

                        @pl.when(g >= 2)
                        def _():
                            rs_copy(g, d, k, h).wait_send()

                    if k < 3 or h == d:
                        for q in (0, 1):
                            ag_copy(g, d, k, h, q).wait_send()
        return 0

    lax.fori_loop(0, NG, left, 0)
    last_sum(NG - 1)

    for n in range(1, NG * SRC):
        back_copy(n // SRC, n % SRC).wait_send()


def shards(tokens, tangent, cotangent, routing, gate_weights, gate_proj, up_proj, down_proj):
    dma = pltpu.SemaphoreType.DMA
    anywhere = pl.BlockSpec(memory_space=pl.ANY)
    vmem = pl.BlockSpec(memory_space=pltpu.VMEM)
    return pl.pallas_call(
        kernel,
        out_shape=jax.ShapeDtypeStruct((TOK, DC), F32),
        in_specs=[anywhere] * 3 + [vmem] * 2 + [anywhere] * 3,
        out_specs=vmem,
        scratch_shapes=[
            pltpu.VMEM((DC, H), BF16),
            pltpu.VMEM((DC, H), BF16),
            pltpu.VMEM((H, DC), BF16),
            pltpu.VMEM((NG, 2, 4, BR, DC), BF16),
            pltpu.VMEM((2, 3 * GR, DC), BF16),
            pltpu.VMEM((5, SUMS * GR, CH), F32),
            pltpu.VMEM((32, MR, 128), jnp.int16),
            pltpu.VMEM((64, MR, 128), jnp.int16),
            pltpu.VMEM((NG * 16, 2 * GR, 128), BF16),
            pltpu.VMEM((GR, DC), F32),
            pltpu.VMEM((NG * SRC, PAD, DC), BF16),
            pltpu.VMEM((32, PAD, DC), BF16),
            pltpu.VMEM((3 * TOK, 32 * PAD), BF16),
            pltpu.VMEM((SRC, NEAR, DC), BF16),
            pltpu.VMEM((SRC, NEAR, DC), BF16),
            dma((3,)), dma((3,)), dma((8,)), dma((8,)), dma((4,)), dma((4,)), dma((8,)), dma((8,)), dma((4,)), dma((4,)),
            dma((16,)), dma((16,)), dma((32,)), dma((64,)), dma((128,)), dma((128,)), dma((32,)), dma((32,)),
        ],
        compiler_params=pltpu.CompilerParams(
            collective_id=0, has_side_effects=True, vmem_limit_bytes=61 * 1024 * 1024
        ),
        cost_estimate=pl.CostEstimate(
            flops=2 * 7 * 576 * DC * H, bytes_accessed=12_000_000, transcendentals=576 * H // NZ
        ),
    )(tokens, tangent, cotangent, routing.T, gate_weights.T, gate_proj[0], up_proj[0], down_proj[0])


def solution(mesh):
    in_specs = (
        P("expert", "dp"),
        P("expert", "dp"),
        P("expert", "dp"),
        P("expert", None),
        P("expert", None),
        P("expert", "dp", None),
        P("expert", "dp", None),
        P("expert", None, "dp"),
    )
    return jax.shard_map(
        shards, mesh=mesh, in_specs=in_specs, out_specs=P("expert", "dp"), check_vma=False
    )
```

```python
import jax
import jax.numpy as jnp
from jax import lax
from jax.experimental import pallas as pl
from jax.experimental.pallas import tpu as pltpu
from jax.sharding import PartitionSpec as P

MESH = pl.DeviceIdType.MESH
BF16 = jnp.bfloat16
F32 = jnp.float32

TOP = 8
TOK = 64
CAP = 18
DC = 896
H = 2048
NZ = 8
CH = H // NZ
NG = 4
SRC = 8
GR = SRC * CAP
SUMS = 5
CHIPS = (
    ((0, 0), (0, 1), (1, 0), (0, 3)),
    ((3, 0), (0, 2), (2, 0), (3, 2)),
    ((1, 2), (2, 1), (2, 3), (2, 2)),
    ((1, 1), (1, 3), (3, 1), (3, 3)),
)
MR = SUMS * GR + 16
BR = 16 + 3 * TOK
PARTS = (pl.ds(0, 16 + TOK), pl.ds(16 + TOK, 2 * TOK))
PAD = 32


def nt(a, b):
    return lax.dot_general(a, b, (((1,), (1,)), ((), ())), preferred_element_type=F32)


def nn(a, b):
    return jnp.dot(a, b, preferred_element_type=F32)


def kernel(
    x_ref, v_ref, c_ref, routing_ref, gw_ref, gate_ref, up_ref, down_ref, out_ref,
    gate_v, up_v, down_v, tok, xrows, part, rs_s, rs_r, fac, acc, sbuf, rbuf, wmat,
    w_sem, l_sem, y_ss, y_rs, x_ss, x_rs, x3_ss, x3_rs, sib_ss, sib_rs,
    rs_ss, rs_rs, ag_ss, ag_rs, rt_ss, rt_rs,
):
    me = lax.axis_index("dp")
    ex = lax.axis_index("expert")
    px = ex // 8
    py = (ex // 2) % 4
    pc = ex % 2

    def at_xy(dx, dy, dc):
        return (me, (((px + dx + 4) % 4) * 4 + (py + dy + 4) % 4) * 2 + (pc + dc) % 2)

    z_dev = ((me + NZ - 1) % NZ, ex), ((me + 1) % NZ, ex)
    y_dev = at_xy(0, 1, 0), at_xy(0, 3, 0)
    x_dev = at_xy(1, 0, 0), at_xy(3, 0, 0)
    sib_dev = at_xy(0, 0, 1)

    def remote(src, dst, ss, rs, dev):
        return pltpu.make_async_remote_copy(
            src_ref=src, dst_ref=dst, send_sem=ss, recv_sem=rs, device_id=dev, device_id_type=MESH
        )

    loads = [
        pltpu.make_async_copy(x_ref, tok.at[0, 0, 0, pl.ds(16, TOK)], l_sem.at[0]),
        pltpu.make_async_copy(v_ref, tok.at[0, 0, 0, pl.ds(16 + TOK, TOK)], l_sem.at[1]),
        pltpu.make_async_copy(c_ref, tok.at[0, 0, 0, pl.ds(16 + 2 * TOK, TOK)], l_sem.at[2]),
    ]
    weights = [
        pltpu.make_async_copy(gate_ref, gate_v, w_sem.at[0]),
        pltpu.make_async_copy(up_ref, up_v, w_sem.at[1]),
        pltpu.make_async_copy(down_ref, down_v, w_sem.at[2]),
    ]
    for cp in loads:
        cp.start()
    for cp in weights:
        cp.start()

    bar = pltpu.get_barrier_semaphore()
    for d in (0, 1):
        pl.semaphore_signal(bar, 1, device_id=z_dev[d], device_id_type=MESH)

    def greet(o, _):
        pl.semaphore_signal(bar, 1, device_id=(me, (ex + o) % 32), device_id_type=MESH)
        return 0

    lax.fori_loop(1, 32, greet, 0)

    named = jnp.concatenate([routing_ref[...].astype(F32), jnp.full((8, TOK), -1.0, F32)], axis=0).astype(BF16)
    twice = lax.broadcasted_iota(jnp.int32, (TOK, 128), 1) % TOK == lax.broadcasted_iota(jnp.int32, (TOK, 128), 0)
    tok[0, 0, 0, pl.ds(0, 16), :] = jnp.zeros((16, DC), BF16)
    tok[0, 0, 0, pl.ds(0, 16), pl.ds(0, 128)] = nn(named, jnp.where(twice, 1.0, 0.0).astype(BF16)).astype(BF16)
    pl.semaphore_wait(bar, 33)

    def slot(col, dy):
        return next((g, i) for g in range(NG) for i in range(4) if CHIPS[g][i] == (col, dy))

    def block(col, dy, q=None):
        g, i = slot(col, dy)
        if q is None:
            return tok.at[g, 0, i]
        return tok.at[g, 0, i, PARTS[q]]

    def y_copy(i, q):
        if i == 0:
            return remote(block(0, 0, q), block(0, 3, q), y_ss.at[q], y_rs.at[q], y_dev[0])
        if i == 1:
            return remote(block(0, 0, q), block(0, 1, q), y_ss.at[2 + q], y_rs.at[2 + q], y_dev[1])
        src = block(0, 3, q) if q == 0 else block(0, 1, q)
        return remote(src, block(0, 2, q), y_ss.at[4 + q], y_rs.at[4 + q], y_dev[q])

    def x_copy(d, dy, q=None):
        i = d * 5 + (dy if dy else 4 * (q or 0))
        return remote(block(0, dy, q), block(1 if d else 3, dy, q), x_ss.at[i], x_rs.at[i], x_dev[d])

    def x3_copy(dy):
        col, d = (1, 1) if dy < 2 else (3, 0)
        return remote(block(col, dy), block(2, dy), x3_ss.at[dy], x3_rs.at[dy], x_dev[d])

    def sib_copy(g, i, q=None):
        n = g * 4 + i + (16 if q == 1 else 0)
        rows = pl.ds(0, BR) if q is None else PARTS[q]
        return remote(tok.at[g, 0, i, rows], tok.at[g, 1, i, rows], sib_ss.at[n], sib_rs.at[n], sib_dev)

    def rs_copy(g, d, k, h):
        s = (((g % 2) * 2 + d) * 4 + k) * 2 + h
        r = ((g * 2 + d) * 4 + k) * 2 + h
        return remote(rs_s.at[s], rs_r.at[r], rs_ss.at[s], rs_rs.at[r], z_dev[d])

    def ag_copy(g, d, k, h, q):
        i = (((g * 2 + d) * 4 + k) * 2 + h) * 2 + q
        src, dst = (k, k + 1) if d == 0 else ((8 - k) % 8, 7 - k)
        rows = pl.ds(q * GR, GR)
        return remote(
            fac.at[(g * 8 + src) * 2 + h, rows], fac.at[(g * 8 + dst) * 2 + h, rows], ag_ss.at[i], ag_rs.at[i], z_dev[d]
        )

    def back_copy(g, j):
        dx, dy = CHIPS[g][j % 4]
        n = g * SRC + j
        return remote(sbuf.at[n], rbuf.at[n], rt_ss.at[n], rt_rs.at[n], at_xy(dx, dy, j // 4))

    def gather(g):
        lane = lax.broadcasted_iota(jnp.int32, (8, 128), 1)
        tri_r = lax.broadcasted_iota(jnp.int32, (128, 128), 0)
        tri_c = lax.broadcasted_iota(jnp.int32, (128, 128), 1)
        tri = ((tri_r < tri_c) & (tri_r // 64 == tri_c // 64)).astype(F32).astype(BF16)
        row = lax.broadcasted_iota(jnp.int32, (GR, 128), 0).astype(F32)
        low = lax.broadcasted_iota(jnp.int32, (16, 128), 1) < 64
        exf = ex.astype(F32)
        hots = []
        for c in range(2):
            for p in range(2):
                ra = tok[g, c, 2 * p, pl.ds(0, 16), pl.ds(0, 128)].astype(F32)
                rb = tok[g, c, 2 * p + 1, pl.ds(0, 16), pl.ds(0, 128)].astype(F32)
                hit = jnp.where(jnp.where(low, ra, rb) == exf, 1.0, 0.0)
                hit = jnp.broadcast_to(jnp.sum(hit, axis=0, keepdims=True), (8, 128))
                rank = nn(hit.astype(BF16), tri)
                first = (CAP * (4 * c + 2 * p) + CAP * (lane // 64)).astype(F32)
                target = jnp.where(hit > 0.5, rank + first, -1.0)
                hots.append(jnp.where(row == target[0:1], 1.0, 0.0).astype(BF16))
        hot = jnp.concatenate(hots, axis=1)
        for a in range(3):
            rows = jnp.concatenate(
                [tok[g, c, y, pl.ds(16 + a * TOK, TOK), :] for c in range(2) for y in range(4)], axis=0
            )
            xrows[g % 2, pl.ds(a * GR, GR), :] = nn(hot, rows).astype(BF16)

    def products(g, d, chunk):
        first = pl.multiple_of(chunk * CH, CH)
        cols = pl.ds(first, CH)
        xv = xrows[g % 2, pl.ds(0, 2 * GR), :]
        part[d, pl.ds(0, 2 * GR), :] = nn(xv, gate_v[:, cols])
        part[d, pl.ds(2 * GR, 2 * GR), :] = nn(xv, up_v[:, cols])
        part[d, pl.ds(4 * GR, GR), :] = nt(xrows[g % 2, pl.ds(2 * GR, GR), :], down_v[cols, :])

    def scales(r):
        return jnp.exp2(rs_r[r, pl.ds(SUMS * GR, 16), :].astype(F32) * (1.0 / 256.0))

    def send_sums(g, d, k, h, came):
        s = (((g % 2) * 2 + d) * 4 + k) * 2 + h
        own = 2 if k == 0 else 3 + d if k == 1 else d

        @pl.when(g >= 2)
        def _():
            rs_copy(g, d, k, h).wait_send()

        r = ((g * 2 + d) * 4 + k - 1) * 2 + h
        if came:
            rs_copy(g, d, k - 1, h).wait_recv()
            sc = scales(r)
        codes = jnp.zeros((16, 128), F32)
        at = lax.broadcasted_iota(jnp.int32, (16, 128), 0)
        for p in range(SUMS):
            rows = pl.ds(p * GR, GR)
            blk = part[own, rows, pl.ds(h * 128, 128)]
            if came:
                blk = blk + rs_r[r, rows, :].astype(F32) * sc[p : p + 1]
            most = jnp.max(jnp.abs(blk), axis=0, keepdims=True)
            code = jnp.ceil(256.0 * jnp.log2(jnp.maximum(most, 1e-30) * (1.0 / 32760.0)))
            inv = jnp.exp2(code * (-1.0 / 256.0))
            rs_s[s, rows, :] = jnp.round(blk * inv).astype(jnp.int32).astype(jnp.int16)
            codes = jnp.where(at == p, code, codes)
        rs_s[s, pl.ds(SUMS * GR, 16), :] = codes.astype(jnp.int32).astype(jnp.int16)
        rs_copy(g, d, k, h).start()

    def stage_0(g):
        products(g, 2, (me + 4) % NZ)
        for d in (0, 1):
            send_sums(g, d, 0, d, False)
        products(g, 3, (me + NZ - 3) % NZ)
        products(g, 4, (me + 3) % NZ)
        for d in (0, 1):
            send_sums(g, d, 1, 1 - d, False)

    def stage(g, k):
        if k == 1:
            for d in (0, 1):
                send_sums(g, d, 1, d, True)
            return
        products(g, 0, (me + NZ - (4 - k)) % NZ)
        products(g, 1, (me + 4 - k) % NZ)
        for h in (1, 0):
            for d in (0, 1):
                send_sums(g, d, k, h if d == 0 else 1 - h, True)

    def stage_4(g):
        products(g, 2, me)
        for h in (0, 1):
            total = []
            r = [((g * 2 + d) * 4 + 3) * 2 + h for d in (0, 1)]
            for d in (0, 1):
                rs_copy(g, d, 3, h).wait_recv()
            sc = [scales(r[0]), scales(r[1])]
            for p in range(SUMS):
                rows = pl.ds(p * GR, GR)
                blk = part[2, rows, pl.ds(h * 128, 128)]
                for d in (0, 1):
                    blk = blk + rs_r[r[d], rows, :].astype(F32) * sc[d][p : p + 1]
                total.append(blk)
            a, da, b, db, dh = total
            sig = 1.0 / (1.0 + jnp.exp(-a))
            s1 = sig * (1.0 + a * (1.0 - sig))
            s2 = sig * (1.0 - sig) * (2.0 + a * (1.0 - 2.0 * sig))
            fac[g * 16 + h, pl.ds(0, GR), :] = (dh * (s2 * da * b + s1 * db)).astype(BF16)
            fac[g * 16 + h, pl.ds(GR, GR), :] = (dh * s1 * da).astype(BF16)
            for q in (0, 1):
                for d in (0, 1):
                    ag_copy(g, d, 0, h, q).start()

    def add_rows(g, r, new):
        cols = pl.ds(pl.multiple_of(((me + r) % NZ) * CH, CH), CH)
        f = jnp.concatenate([fac[(g * 8 + r) * 2], fac[(g * 8 + r) * 2 + 1]], axis=1)
        more = nt(f[0:GR], gate_v[:, cols]) + nt(f[GR:], up_v[:, cols])
        acc[...] = more if new else acc[...] + more

    def gather_stage(g, k):
        for h in (0, 1):
            for q in (0, 1):
                for d in (0, 1):
                    ag_copy(g, d, k - 1, h, q).wait_recv()
                    if k < 3 or h == d:
                        ag_copy(g, d, k, h, q).start()
        if k == 1:
            add_rows(g, 0, True)
        add_rows(g, k, False)
        add_rows(g, 8 - k, False)

    def last_stage(g):
        for q in (0, 1):
            for d in (0, 1):
                ag_copy(g, d, 3, d, q).wait_recv()
        add_rows(g, 4, False)
        rows = acc[...].astype(BF16)
        o = lax.broadcasted_iota(jnp.int32, (SRC * PAD, GR), 0)
        i = lax.broadcasted_iota(jnp.int32, (SRC * PAD, GR), 1)
        hot = jnp.where((o % PAD < CAP) & (i == (o // PAD) * CAP + o % PAD), 1.0, 0.0).astype(BF16)
        spread = nn(hot, rows).astype(BF16)
        for j in range(SRC):
            sbuf[g * SRC + j] = spread[j * PAD : (j + 1) * PAD]
        for at in range(NG):

            @pl.when(g == at)
            def _():
                for j in range(SRC):
                    if at == 0 and j == 0:
                        pltpu.make_async_copy(sbuf.at[0], rbuf.at[0], rt_rs.at[0]).start()
                    else:
                        back_copy(at, j).start()

    loads[0].wait()
    for q in (0, 1):
        if q == 1:
            loads[1].wait()
            loads[2].wait()
        y_copy(0, q).start()
        y_copy(1, q).start()
        x_copy(1, 0, q).start()
        sib_copy(0, 0, q).start()
        x_copy(0, 0, q).start()

    same = lax.broadcasted_iota(jnp.int32, (TOK, TOK), 0) == lax.broadcasted_iota(jnp.int32, (TOK, TOK), 1)
    same = jnp.where(same, 1.0, 0.0).astype(BF16)
    names = nt(same, routing_ref[...].astype(F32).astype(BF16))
    rest = gw_ref[...]
    gw = jnp.zeros((TOK, TOP), F32)
    for i in range(3):
        piece = rest.astype(BF16)
        gw = gw + nt(same, piece)
        rest = rest - piece.astype(F32)
    hits = jnp.zeros((TOK, 128), F32)
    lane = lax.broadcasted_iota(jnp.int32, (TOK, 128), 1).astype(F32)
    for k in range(TOP):
        hits = hits + jnp.where(names[:, k : k + 1] == lane, 1.0, 0.0)
    order = jnp.zeros((TOK, 128), F32)
    for n in range(NG * SRC):
        dx, dy = CHIPS[n // SRC][n % 4]
        order = jnp.where(lane == at_xy(-dx, -dy, n % SRC // 4)[1].astype(F32), float(n), order)
    tri = lax.broadcasted_iota(jnp.int32, (TOK, TOK), 1) < lax.broadcasted_iota(jnp.int32, (TOK, TOK), 0)
    place = nn(jnp.where(tri, 1.0, 0.0).astype(BF16), hits.astype(BF16)) + order * PAD
    col = lax.broadcasted_iota(jnp.int32, (TOK, 32 * PAD), 1).astype(F32)
    w = jnp.zeros((TOK, 32 * PAD), F32)
    for k in range(TOP):
        at = jnp.sum(jnp.where(names[:, k : k + 1] == lane, place, 0.0), axis=1, keepdims=True)
        w = w + jnp.where(col == at, gw[:, k : k + 1], 0.0)
    for i in range(3):
        piece = w.astype(BF16)
        wmat[pl.ds(i * TOK, TOK), :] = piece
        w = w - piece.astype(F32)

    for q in (0, 1):
        y_copy(1, q).wait_recv()
        sib_copy(0, 1, q).start()
        x_copy(1, 0, q).wait_recv()
        sib_copy(0, 2, q).start()
        y_copy(0, q).wait_recv()
        sib_copy(0, 3, q).start()
        y_copy(2, q).start()
    x3_copy(0).start()
    for cp in weights:
        cp.wait()
    for q in (0, 1):
        for i in range(4):
            sib_copy(0, i, q).wait_recv()
    gather(0)
    stage_0(0)
    for q in (0, 1):
        y_copy(2, q).wait_recv()
    for dy in (2, 1, 3):
        for d in (0, 1):
            x_copy(d, dy).start()
    sib_copy(1, 1).start()
    stage(0, 1)

    def last_sum(g):
        for j in range(SRC):
            n = g * SRC + j
            pltpu.make_async_copy(rbuf.at[n], rbuf.at[n], rt_rs.at[n]).wait()
        rows = rbuf[pl.ds(g * SRC, SRC)].reshape(SRC * PAD, DC)
        parts = nn(wmat[:, pl.ds(g * SRC * PAD, SRC * PAD)], rows)
        parts = parts[2 * TOK :] + parts[TOK : 2 * TOK] + parts[:TOK]
        out_ref[...] = parts if g == 0 else out_ref[...] + parts

    def turn(i, _):
        factors = (i >= 1) & (i <= NG)

        @pl.when(i < NG)
        def _():
            stage(i, 2)

        @pl.when(i == NG + 1)
        def _():
            for g in range(NG - 1):
                last_sum(g)

        @pl.when(i >= 2)
        def _():
            last_stage(i - 2)

        @pl.when(i == 0)
        def _():
            stage(0, 3)
            for q in (0, 1):
                x_copy(0, 0, q).wait_recv()
            sib_copy(1, 0).start()
            x3_copy(0).wait_recv()
            sib_copy(1, 2).start()
            x_copy(0, 2).wait_recv()
            sib_copy(1, 3).start()
            x3_copy(2).start()
            for j in range(4):
                sib_copy(1, j).wait_recv()

        @pl.when(i == 1)
        def _():
            for dy in (1, 3, 2):
                x3_copy(dy).wait_recv()
                sib_copy(2, slot(2, dy)[1]).start()
            for j in range(4):
                sib_copy(2, j).wait_recv()

        @pl.when(i == 2)
        def _():
            for j in range(4):
                sib_copy(3, j).wait_recv()

        @pl.when(i < NG - 1)
        def _():
            gather(i + 1)
            stage_0(i + 1)

        @pl.when(factors)
        def _():
            gather_stage(i - 1, 1)

        @pl.when((i > 0) & (i < NG))
        def _():
            stage(i, 3)

        @pl.when(factors)
        def _():
            gather_stage(i - 1, 2)

        @pl.when(i < NG - 1)
        def _():
            stage(i + 1, 1)

        @pl.when(i == 0)
        def _():
            x_copy(0, 3).wait_recv()
            x3_copy(3).start()
            x_copy(1, 1).wait_recv()
            x3_copy(1).start()
            x_copy(1, 2).wait_recv()
            sib_copy(2, 0).start()
            x_copy(1, 3).wait_recv()
            x_copy(0, 1).wait_recv()
            for j in range(4):
                sib_copy(3, j).start()

        @pl.when(i < NG)
        def _():
            stage_4(i)

        @pl.when(factors)
        def _():
            gather_stage(i - 1, 3)

        return 0

    lax.fori_loop(0, NG + 2, turn, 0)

    for q in (0, 1):
        for i in range(3):
            y_copy(i, q).wait_send()
        for d in (0, 1):
            x_copy(d, 0, q).wait_send()
        for i in range(4):
            sib_copy(0, i, q).wait_send()
    for i in range(4):
        x3_copy(i).wait_send()
        for g in range(1, NG):
            sib_copy(g, i).wait_send()
        for d in (0, 1):
            if i:
                x_copy(d, i).wait_send()

    def left(g, _):
        for d in (0, 1):
            for k in range(4):
                for h in (0, 1):
                    if k > 0 or h == d:

                        @pl.when(g >= 2)
                        def _():
                            rs_copy(g, d, k, h).wait_send()

                    if k < 3 or h == d:
                        for q in (0, 1):
                            ag_copy(g, d, k, h, q).wait_send()
        return 0

    lax.fori_loop(0, NG, left, 0)
    last_sum(NG - 1)

    for n in range(1, NG * SRC):
        back_copy(n // SRC, n % SRC).wait_send()


def shards(tokens, tangent, cotangent, routing, gate_weights, gate_proj, up_proj, down_proj):
    dma = pltpu.SemaphoreType.DMA
    anywhere = pl.BlockSpec(memory_space=pl.ANY)
    vmem = pl.BlockSpec(memory_space=pltpu.VMEM)
    return pl.pallas_call(
        kernel,
        out_shape=jax.ShapeDtypeStruct((TOK, DC), F32),
        in_specs=[anywhere] * 3 + [vmem] * 2 + [anywhere] * 3,
        out_specs=vmem,
        scratch_shapes=[
            pltpu.VMEM((DC, H), BF16),
            pltpu.VMEM((DC, H), BF16),
            pltpu.VMEM((H, DC), BF16),
            pltpu.VMEM((NG, 2, 4, BR, DC), BF16),
            pltpu.VMEM((2, 3 * GR, DC), BF16),
            pltpu.VMEM((5, SUMS * GR, CH), F32),
            pltpu.VMEM((32, MR, 128), jnp.int16),
            pltpu.VMEM((64, MR, 128), jnp.int16),
            pltpu.VMEM((NG * 16, 2 * GR, 128), BF16),
            pltpu.VMEM((GR, DC), F32),
            pltpu.VMEM((NG * SRC, PAD, DC), BF16),
            pltpu.VMEM((32, PAD, DC), BF16),
            pltpu.VMEM((3 * TOK, 32 * PAD), BF16),
            dma((3,)), dma((3,)), dma((6,)), dma((6,)), dma((10,)), dma((10,)), dma((4,)), dma((4,)),
            dma((20,)), dma((20,)), dma((32,)), dma((64,)), dma((128,)), dma((128,)), dma((32,)), dma((32,)),
        ],
        compiler_params=pltpu.CompilerParams(
            collective_id=0, has_side_effects=True, vmem_limit_bytes=61 * 1024 * 1024
        ),
        cost_estimate=pl.CostEstimate(
            flops=2 * 7 * 576 * DC * H, bytes_accessed=12_000_000, transcendentals=576 * H // NZ
        ),
    )(tokens, tangent, cotangent, routing.T, gate_weights.T, gate_proj[0], up_proj[0], down_proj[0])


def solution(mesh):
    in_specs = (
        P("expert", "dp"),
        P("expert", "dp"),
        P("expert", "dp"),
        P("expert", None),
        P("expert", None),
        P("expert", "dp", None),
        P("expert", "dp", None),
        P("expert", None, "dp"),
    )
    return jax.shard_map(
        shards, mesh=mesh, in_specs=in_specs, out_specs=P("expert", "dp"), check_vma=False
    )
```
